32 devices in a mesh: sta: 8 (over y, x, core), tm: 4 (over z).
Axes of the slice: x: 2, y: 2, z: 4, core: 2. Of those that a mesh axis runs over, the one named last changes fastest.
Arguments:
- records: bfloat16 [1024, 1024], P('sta', 'tm'), may hold values from -6 to 6
- filter_taps: float32 [127], replicated, may hold values from -0.5 to 0.5
- plan: int32 [3], replicated, may hold values from 1 to 7, as said below
- station_valid: int32 [1024], P('sta'), may hold values 0 or 1
Outputs:
- correlations: bfloat16 [3, 1024, 101, 128], P(None, ('sta', 'tm'))
The draws below stay inside these ranges and needn't reach their ends.
Inputs may be any that keep to these rules, and one draw needn't show every extreme that they name: `plan`: the 3 distances are distinct, and one of them is 7.
All inputs are finite; a program needn't handle non-finite values. No bound on the sum of `station_valid` on one device may be relied on, other than what follows from the above.
Results may differ from the reference program's by a relative error of at most 0.0048.
Values may be sent and summed in bfloat16 or wider, within the bound.
A program may use at most 64 MiB of HBM per device.

```python
import jax
import jax.numpy as jnp
from jax import lax

STA_DEV = 128
SAMPLES = 1024
TAPS = 127
AVG_HALF = 64
LAGS = 101
ROUNDS = 3
BLOCKS = 8
STATIONS = 1024


def draw_plan(key, part):
    first_key = jax.random.fold_in(key, 11)
    second_key = jax.random.fold_in(key, 23)
    shuffled = jax.random.permutation(first_key, BLOCKS - 2) + 1
    chosen = jnp.concatenate([jnp.array([BLOCKS - 1], jnp.int32), shuffled[:ROUNDS - 1].astype(jnp.int32)])
    placing = jax.random.permutation(second_key, ROUNDS)
    return chosen[placing].astype(jnp.int32)


def with_ends(values, own_key, smallest, largest):
    longest = values.shape.index(max(values.shape))
    spots = []
    for shift in (0, 1):
        where = [jax.random.randint(jax.random.fold_in(own_key, axis), (), 0, length) for axis, length in enumerate(values.shape)]
        where[longest] = (where[longest] + shift) % values.shape[longest]
        spots.append(tuple(where))
    return values.at[spots[0]].set(smallest).at[spots[1]].set(largest)


def block_levels(key, shape, split, least, high):
    gain = 1.0
    for position, blocks in split:
        heights = jax.random.uniform(jax.random.fold_in(jax.random.fold_in(key, 6), position), (blocks,), jnp.float32, least / len(split), high / len(split))
        gain = gain * jnp.repeat(jnp.exp(heights), shape[position] // blocks).reshape((-1,) + (1,) * (len(shape) - 1 - position))
    return gain


def normal_values(rng, extent, scale, most, cuts=(), held_as=jnp.bfloat16):
    drawn = scale * jax.random.normal(rng, extent, jnp.float32)
    if cuts:
        drawn = drawn * block_levels(rng, extent, cuts, -0.22, 0.18)
    return jnp.clip(drawn, -most, most).astype(held_as)


def setup_inputs(seed: int = 0) -> dict:
    key_list = jax.random.split(jax.random.key(seed), 5)
    return {
        "records": normal_values(key_list[0], (STATIONS, SAMPLES), 1.0, 6.0, ((0, 8), (1, 4))),
        "filter_taps": normal_values(key_list[1], (TAPS,), TAPS ** -0.5, 0.5, (), jnp.float32),
        "plan": draw_plan(jax.random.fold_in(key_list[4], 71), 0),
        "station_valid": with_ends((jax.random.randint(key_list[3], (STATIONS,), 0, 8) < 7).astype(jnp.int32), jax.random.fold_in(key_list[3], 1), 0, 1),
    }


def reference(records, filter_taps, plan, station_valid):
    half_taps = (TAPS - 1) // 2
    half_lags = (LAGS - 1) // 2
    signal = records.astype(jnp.float32)
    padded = jnp.pad(signal, ((0, 0), (half_taps, half_taps)))
    filtered = jnp.zeros_like(signal)
    for k in range(TAPS):
        filtered = filtered + filter_taps[k] * padded[:, k:k + SAMPLES]
    magnitude_pad = jnp.pad(jnp.abs(filtered), ((0, 0), (AVG_HALF, AVG_HALF)))
    magnitude_sum = lax.reduce_window(magnitude_pad, jnp.zeros((), filtered.dtype), lax.add, (1, 2 * AVG_HALF + 1), (1, 1), 'VALID')
    magnitude = magnitude_sum / (2 * AVG_HALF + 1) + 1e-05
    normalized = (filtered / magnitude * station_valid[:, None].astype(jnp.float32)).astype(jnp.bfloat16)
    blocks = normalized.astype(jnp.float32).reshape(BLOCKS, STA_DEV, SAMPLES)
    padded_blocks = jnp.pad(blocks, ((0, 0), (0, 0), (half_lags, half_lags)))
    factor = 1.0 / jnp.sqrt(jnp.float32(SAMPLES))

    def one_round(distance):

        def one_block(index):
            own_rows = blocks[index]
            partner = padded_blocks[jnp.bitwise_xor(index, distance)]
            windows = jnp.stack([partner[:, l:l + SAMPLES] for l in range(LAGS)])
            return jnp.einsum('it,ljt->ilj', own_rows, windows, precision=lax.Precision.HIGHEST)
        values = lax.map(one_block, jnp.arange(BLOCKS, dtype=jnp.int32))
        return (values.reshape(STATIONS, LAGS, STA_DEV) * factor).astype(jnp.bfloat16)
    results = [one_round(plan[r].astype(jnp.int32)) for r in range(ROUNDS)]
    return jnp.stack(results)
```

```python
import functools

import jax
import jax.numpy as jnp
from jax import lax
from jax.experimental import pallas as pl
from jax.experimental.pallas import tpu as pltpu
from jax.sharding import PartitionSpec as P

AVG_HALF = 64
LAGS = 101
ROUNDS = 3
TILE = 256
EDGE = 128
LAG_GROUP = 26
MESH = pl.DeviceIdType.MESH


def flipped(index, mask):
    bit = 1
    while bit <= mask:
        if mask & bit:
            index = index + bit - 2 * bit * (lax.div(index, bit) % 2)
        bit *= 2
    return index


def gather_kernel(n_sta, n_tm, valid_ref, rec_ref, all_ref, masked, keep_sem, z_send, z_recv, send, recv):
    sta = lax.axis_index("sta")
    tm = lax.axis_index("tm")
    bits = n_sta.bit_length() - 1
    offsets = sorted(range(1, n_tm), key=lambda k: (min(k, n_tm - k), k))

    def tm_at(k):
        return lax.rem(tm + k, n_tm)

    barrier = pltpu.get_barrier_semaphore()
    for b in range(bits):
        pl.semaphore_signal(barrier, inc=1, device_id=(flipped(sta, 1 << b), tm), device_id_type=MESH)
    for k in offsets:
        pl.semaphore_signal(barrier, inc=1, device_id=(sta, tm_at(k)), device_id_type=MESH)

    rows = rec_ref.shape[0]
    row = lax.broadcasted_iota(jnp.int32, (rows, rows), 0)
    col = lax.broadcasted_iota(jnp.int32, (rows, rows), 1)
    keep = jnp.where(row == col, valid_ref[...], 0).astype(jnp.float32).astype(jnp.bfloat16)
    masked[...] = jnp.dot(keep, rec_ref[...], preferred_element_type=jnp.float32).astype(jnp.bfloat16)
    own_copy = pltpu.make_async_copy(masked, all_ref.at[sta, tm], keep_sem)
    own_copy.start()

    pl.semaphore_wait(barrier, bits + n_tm - 1)
    started = []

    def pass_on(mask, k, b):
        there = (flipped(sta, mask), tm_at(k))
        source = masked if (mask, k) == (0, 0) else all_ref.at[there]
        copy = pltpu.make_async_remote_copy(
            src_ref=source,
            dst_ref=all_ref.at[there],
            send_sem=send.at[mask ^ (1 << b), k],
            recv_sem=recv.at[mask ^ (1 << b), k],
            device_id=(flipped(sta, 1 << b), tm),
            device_id_type=MESH,
        )
        copy.start()
        started.append(copy)

    for k in offsets:
        copy = pltpu.make_async_remote_copy(
            src_ref=masked,
            dst_ref=all_ref.at[sta, tm],
            send_sem=z_send.at[k],
            recv_sem=z_recv.at[n_tm - k],
            device_id=(sta, tm_at(k)),
            device_id_type=MESH,
        )
        copy.start()
        started.append(copy)

    def arrival(ref_sem, mask, k):
        there = all_ref.at[flipped(sta, mask), tm_at(k)]
        pltpu.make_async_copy(there, there, ref_sem).wait()

    def dims(position):
        outer = list(range(1, bits))
        turn = position % len(outer) if outer else 0
        return outer[turn:] + outer[:turn]

    def own_ready(position, k):
        if k:
            arrival(z_recv.at[k], 0, k)
        for b in dims(position):
            pass_on(0, k, b)
        if bits:
            pass_on(0, k, 0)

    def forward(position, k, level):
        order = dims(position)
        for sub in range(1 << level):
            mask = 1 << order[level]
            for a in range(level):
                if sub >> a & 1:
                    mask |= 1 << order[a]
            arrival(recv.at[mask, k], mask, k)
            for b in order[level + 1:]:
                pass_on(mask, k, b)
            pass_on(mask, k, 0)

    chunks = [0] + offsets
    levels = max(bits - 1, 0)
    for turn in range(len(chunks) + levels):
        for level in range(levels, -1, -1):
            position = turn - level
            if 0 <= position < len(chunks):
                if level == 0:
                    own_ready(position, chunks[position])
                else:
                    forward(position, chunks[position], level - 1)
    for position, k in enumerate(chunks):
        for mask in range(1, n_sta, 2):
            arrival(recv.at[mask, k], mask, k)
    for copy in started:
        copy.wait_send()
    own_copy.wait()


def gather(records, valid, n_sta, n_tm):
    rows, cols = records.shape
    return pl.pallas_call(
        functools.partial(gather_kernel, n_sta, n_tm),
        out_shape=jax.ShapeDtypeStruct((n_sta, n_tm, rows, cols), records.dtype),
        in_specs=[pl.BlockSpec(memory_space=pltpu.VMEM)] * 2,
        out_specs=pl.BlockSpec(memory_space=pl.ANY),
        scratch_shapes=[
            pltpu.VMEM((rows, cols), records.dtype),
            pltpu.SemaphoreType.DMA,
            pltpu.SemaphoreType.DMA((n_tm,)),
            pltpu.SemaphoreType.DMA((n_tm,)),
            pltpu.SemaphoreType.DMA((n_sta, n_tm)),
            pltpu.SemaphoreType.DMA((n_sta, n_tm)),
        ],
        compiler_params=pltpu.CompilerParams(collective_id=0, has_side_effects=True),
        name="gather_records",
    )(valid, records)


def times_rows(left, right):
    return lax.dot_general(left, right, (((1,), (1,)), ((), ())), preferred_element_type=jnp.float32)


def correlate_kernel(n_tm, where_ref, taps_ref, all_ref, out_ref, raw, tapline, filt, high, low, partners, own, toep, stage, in_sem, out_sem):
    block_rows, cols = all_ref.shape[2], all_ref.shape[3]
    length = n_tm * cols
    own_rows = own.shape[0]
    n_taps = taps_ref.shape[1]
    paired = ROUNDS * block_rows
    copies = []
    for r in range(ROUNDS):
        for c in range(n_tm):
            copies.append(pltpu.make_async_copy(
                all_ref.at[where_ref[r], c],
                raw.at[pl.ds(r * block_rows, block_rows), pl.ds(EDGE + c * cols, cols)],
                in_sem.at[r, c],
            ))
    first = pl.multiple_of(where_ref[ROUNDS + 1] * own_rows, own_rows)
    for c in range(n_tm):
        copies.append(pltpu.make_async_copy(
            all_ref.at[where_ref[ROUNDS], c, pl.ds(first, own_rows), :],
            raw.at[pl.ds(paired, own_rows), pl.ds(EDGE + c * cols, cols)],
            in_sem.at[ROUNDS, c],
        ))
    for copy in copies:
        copy.start()

    for ref in (raw, high, low, own):
        blank = jnp.zeros((ref.shape[0], EDGE), ref.dtype)
        ref[:, :EDGE] = blank
        ref[:, EDGE + length:] = blank
    span = TILE + 2 * EDGE
    tapline[...] = jnp.zeros(tapline.shape, tapline.dtype)
    tapline[0:1, :n_taps] = taps_ref[...]
    line = jnp.broadcast_to(tapline[0:1, :], (TILE, span))
    band = pltpu.roll(line, EDGE - (n_taps - 1) // 2, 1, stride=1, stride_axis=0)
    band_high = band.astype(jnp.bfloat16)
    band_low = (band - band_high.astype(jnp.float32)).astype(jnp.bfloat16)
    ahead = lax.broadcasted_iota(jnp.int32, (TILE, span), 1) - lax.broadcasted_iota(jnp.int32, (TILE, span), 0) - EDGE
    box = jnp.where((ahead >= -AVG_HALF) & (ahead <= AVG_HALF), 1.0, 0.0).astype(jnp.bfloat16)

    for copy in copies:
        copy.wait()
    for t in range(0, length, TILE):
        window = raw[:, t:t + span]
        value = times_rows(window, band_high) + times_rows(window, band_low)
        filt[:, t:t + TILE] = value
        size = jnp.abs(value)
        top = size.astype(jnp.bfloat16)
        high[:, EDGE + t:EDGE + t + TILE] = top
        low[:, EDGE + t:EDGE + t + TILE] = (size - top.astype(jnp.float32)).astype(jnp.bfloat16)
    for t in range(0, length, TILE):
        total = times_rows(high[:, t:t + span], box) + times_rows(low[:, t:t + span], box)
        magnitude = total * (1.0 / (2 * AVG_HALF + 1)) + 1e-5
        normal = (filt[:, t:t + TILE] / magnitude).astype(jnp.bfloat16)
        partners[:, t:t + TILE] = normal[:paired]
        own[:, EDGE + t:EDGE + t + TILE] = normal[paired:]

    factor = float(length) ** -0.5
    half_lags = (LAGS - 1) // 2
    own_wide = own[...]
    results = []
    for g, l0 in enumerate(range(0, LAGS, LAG_GROUP)):
        count = min(LAG_GROUP, LAGS - l0)
        for l in range(count):
            begin = EDGE + half_lags - l0 - l
            toep[(l0 + l) * own_rows:(l0 + l + 1) * own_rows, :] = own_wide[:, begin:begin + length]
        rows = toep[l0 * own_rows:(l0 + count) * own_rows, :]
        sums = (times_rows(rows, partners[...]) * factor).astype(jnp.bfloat16)
        for r in range(ROUNDS):
            part = sums[:, r * block_rows:(r + 1) * block_rows]
            stage[r, l0:l0 + count] = part.reshape(count, own_rows, block_rows)
        result = pltpu.make_async_copy(
            stage.at[:, pl.ds(l0, count)], out_ref.at[:, pl.ds(l0, count)], out_sem.at[g]
        )
        result.start()
        results.append(result)
    for result in results:
        result.wait()


def correlate(everything, where, taps):
    n_sta, n_tm, block_rows, cols = everything.shape
    length = n_tm * cols
    own_rows = block_rows // n_tm
    rows = ROUNDS * block_rows + own_rows
    wide = length + 2 * EDGE
    groups = -(-LAGS // LAG_GROUP)
    bf16 = jnp.bfloat16
    return pl.pallas_call(
        functools.partial(correlate_kernel, n_tm),
        out_shape=jax.ShapeDtypeStruct((ROUNDS, LAGS, own_rows, block_rows), bf16),
        in_specs=[
            pl.BlockSpec(memory_space=pltpu.SMEM),
            pl.BlockSpec(memory_space=pltpu.VMEM),
            pl.BlockSpec(memory_space=pl.ANY),
        ],
        out_specs=pl.BlockSpec(memory_space=pl.ANY),
        scratch_shapes=[
            pltpu.VMEM((rows, wide), bf16),
            pltpu.VMEM((8, TILE + 2 * EDGE), jnp.float32),
            pltpu.VMEM((rows, length), jnp.float32),
            pltpu.VMEM((rows, wide), bf16),
            pltpu.VMEM((rows, wide), bf16),
            pltpu.VMEM((ROUNDS * block_rows, length), bf16),
            pltpu.VMEM((own_rows, wide), bf16),
            pltpu.VMEM((LAGS * own_rows, length), bf16),
            pltpu.VMEM((ROUNDS, LAGS, own_rows, block_rows), bf16),
            pltpu.SemaphoreType.DMA((ROUNDS + 1, n_tm)),
            pltpu.SemaphoreType.DMA((groups,)),
        ],
        compiler_params=pltpu.CompilerParams(vmem_limit_bytes=48 * 2**20),
        name="correlate_blocks",
    )(where, taps, everything)


def local(records, filter_taps, plan, station_valid):
    n_sta, n_tm = lax.axis_size("sta"), lax.axis_size("tm")
    everything = gather(records, station_valid[None, :], n_sta, n_tm)
    sta = lax.axis_index("sta").astype(jnp.int32)
    here = jnp.stack([sta, lax.axis_index("tm").astype(jnp.int32)])
    where = jnp.concatenate([jnp.bitwise_xor(plan, sta), here])
    lagged = correlate(everything, where, filter_taps[None, :])
    return jnp.transpose(lagged, (0, 2, 1, 3))


def solution(mesh):
    return jax.shard_map(
        local,
        mesh=mesh,
        in_specs=(P("sta", "tm"), P(), P(), P("sta")),
        out_specs=P(None, ("sta", "tm"), None, None),
        check_vma=False,
    )
```

```python
import functools

import jax
import jax.numpy as jnp
from jax import lax
from jax.experimental import pallas as pl
from jax.experimental.pallas import tpu as pltpu
from jax.sharding import PartitionSpec as P

AVG_HALF = 64
LAGS = 101
ROUNDS = 3
TILE = 256
EDGE = 128
LAG_GROUP = 26
MESH = pl.DeviceIdType.MESH


def flipped(index, mask):
    bit = 1
    while bit <= mask:
        if mask & bit:
            index = index + bit - 2 * bit * (lax.div(index, bit) % 2)
        bit *= 2
    return index


def gather_kernel(n_sta, n_tm, valid_ref, rec_ref, all_ref, masked, keep_sem, z_send, z_recv, send, recv):
    sta = lax.axis_index("sta")
    tm = lax.axis_index("tm")
    bits = n_sta.bit_length() - 1
    outer = list(range(1, bits))

    def chunk_at(position):
        chunk = tm
        for here in range(n_tm):
            near = sorted(range(n_tm), key=lambda there: (abs(there - here), there))
            chunk = jnp.where(tm == here, near[position], chunk)
        return chunk

    chunks = [tm] + [chunk_at(position) for position in range(1, n_tm)]

    barrier = pltpu.get_barrier_semaphore()
    masks = [1] + list(range(2, n_sta, 2))
    for mask in masks:
        pl.semaphore_signal(barrier, inc=1, device_id=(flipped(sta, mask), tm), device_id_type=MESH)
    for chunk in chunks[1:]:
        pl.semaphore_signal(barrier, inc=1, device_id=(sta, chunk), device_id_type=MESH)

    rows = rec_ref.shape[0]
    row = lax.broadcasted_iota(jnp.int32, (rows, rows), 0)
    col = lax.broadcasted_iota(jnp.int32, (rows, rows), 1)
    keep = jnp.where(row == col, valid_ref[...], 0).astype(jnp.float32).astype(jnp.bfloat16)
    masked[...] = jnp.dot(keep, rec_ref[...], preferred_element_type=jnp.float32).astype(jnp.bfloat16)
    own_copy = pltpu.make_async_copy(masked, all_ref.at[sta, tm], keep_sem)
    own_copy.start()

    pl.semaphore_wait(barrier, len(masks) + n_tm - 1)
    started = []

    def pass_on(mask, position, jump):
        there = (flipped(sta, mask), chunks[position])
        copy = pltpu.make_async_remote_copy(
            src_ref=masked if mask == position == 0 else all_ref.at[there],
            dst_ref=all_ref.at[there],
            send_sem=send.at[mask ^ jump, position],
            recv_sem=recv.at[mask ^ jump, position],
            device_id=(flipped(sta, jump), tm),
            device_id_type=MESH,
        )
        copy.start()
        started.append(copy)

    def arrival(sem, mask, position):
        there = all_ref.at[flipped(sta, mask), chunks[position]]
        pltpu.make_async_copy(there, there, sem).wait()

    for position in range(1, n_tm):
        copy = pltpu.make_async_remote_copy(
            src_ref=masked,
            dst_ref=all_ref.at[sta, tm],
            send_sem=z_send.at[position],
            recv_sem=z_recv.at[tm],
            device_id=(sta, chunks[position]),
            device_id_type=MESH,
        )
        copy.start()
        started.append(copy)

    def direct(position):
        return position == n_tm - 1 or len(outer) != 2

    def first_bits(position):
        turn = position % 2
        return outer[turn:] + outer[:turn]

    def own_ready(position):
        if position:
            arrival(z_recv.at[chunks[position]], 0, position)
        if direct(position):
            for mask in range(2, n_sta, 2):
                pass_on(0, position, mask)
        else:
            for b in first_bits(position):
                pass_on(0, position, 1 << b)
        pass_on(0, position, 1)

    def relay(position):
        if not direct(position):
            first, second = first_bits(position)
            arrival(recv.at[1 << first, position], 1 << first, position)
            pass_on(1 << first, position, 1 << second)
            pass_on(1 << first, position, 1)

    for position in range(n_tm + 1):
        if position < n_tm:
            own_ready(position)
        if position:
            relay(position - 1)
    for position in range(n_tm):
        for mask in range(2, n_sta, 2):
            if direct(position) or mask != 1 << first_bits(position)[0]:
                arrival(recv.at[mask, position], mask, position)
                pass_on(mask, position, 1)
    for position in range(n_tm):
        for mask in range(1, n_sta, 2):
            arrival(recv.at[mask, position], mask, position)
    for copy in started:
        copy.wait_send()
    own_copy.wait()


def gather(records, valid, n_sta, n_tm):
    rows, cols = records.shape
    return pl.pallas_call(
        functools.partial(gather_kernel, n_sta, n_tm),
        out_shape=jax.ShapeDtypeStruct((n_sta, n_tm, rows, cols), records.dtype),
        in_specs=[pl.BlockSpec(memory_space=pltpu.VMEM)] * 2,
        out_specs=pl.BlockSpec(memory_space=pl.ANY),
        scratch_shapes=[
            pltpu.VMEM((rows, cols), records.dtype),
            pltpu.SemaphoreType.DMA,
            pltpu.SemaphoreType.DMA((n_tm,)),
            pltpu.SemaphoreType.DMA((n_tm,)),
            pltpu.SemaphoreType.DMA((n_sta, n_tm)),
            pltpu.SemaphoreType.DMA((n_sta, n_tm)),
        ],
        compiler_params=pltpu.CompilerParams(
            collective_id=0, has_side_effects=True, vmem_limit_bytes=60 * 2**20
        ),
        name="gather_records",
    )(valid, records)


def times_rows(left, right):
    return lax.dot_general(left, right, (((1,), (1,)), ((), ())), preferred_element_type=jnp.float32)


def correlate_kernel(n_tm, plan_ref, taps_ref, all_ref, out_ref, raw, tapline, filt, high, low, partners, own, toep, stage, in_sem, out_sem):
    block_rows, cols = all_ref.shape[2], all_ref.shape[3]
    length = n_tm * cols
    own_rows = own.shape[0]
    n_taps = taps_ref.shape[1]
    paired = ROUNDS * block_rows
    sta = lax.axis_index("sta")
    copies = []
    for r in range(ROUNDS):
        for c in range(n_tm):
            copies.append(pltpu.make_async_copy(
                all_ref.at[jnp.bitwise_xor(plan_ref[r], sta), c],
                raw.at[pl.ds(r * block_rows, block_rows), pl.ds(EDGE + c * cols, cols)],
                in_sem.at[r, c],
            ))
    first = pl.multiple_of(lax.axis_index("tm") * own_rows, own_rows)
    for c in range(n_tm):
        copies.append(pltpu.make_async_copy(
            all_ref.at[sta, c, pl.ds(first, own_rows), :],
            raw.at[pl.ds(paired, own_rows), pl.ds(EDGE + c * cols, cols)],
            in_sem.at[ROUNDS, c],
        ))
    for copy in copies:
        copy.start()

    for ref in (raw, high, low, own):
        blank = jnp.zeros((ref.shape[0], EDGE), ref.dtype)
        ref[:, :EDGE] = blank
        ref[:, EDGE + length:] = blank
    span = TILE + 2 * EDGE
    tapline[...] = jnp.zeros(tapline.shape, tapline.dtype)
    tapline[0:1, :n_taps] = taps_ref[...]
    line = jnp.broadcast_to(tapline[0:1, :], (TILE, span))
    band = pltpu.roll(line, EDGE - (n_taps - 1) // 2, 1, stride=1, stride_axis=0)
    band_high = band.astype(jnp.bfloat16)
    band_low = (band - band_high.astype(jnp.float32)).astype(jnp.bfloat16)
    ahead = lax.broadcasted_iota(jnp.int32, (TILE, span), 1) - lax.broadcasted_iota(jnp.int32, (TILE, span), 0) - EDGE
    box = jnp.where((ahead >= -AVG_HALF) & (ahead <= AVG_HALF), 1.0, 0.0).astype(jnp.bfloat16)

    for copy in copies:
        copy.wait()
    for t in range(0, length, TILE):
        window = raw[:, t:t + span]
        value = times_rows(window, band_high) + times_rows(window, band_low)
        filt[:, t:t + TILE] = value
        size = jnp.abs(value)
        top = size.astype(jnp.bfloat16)
        high[:, EDGE + t:EDGE + t + TILE] = top
        low[:, EDGE + t:EDGE + t + TILE] = (size - top.astype(jnp.float32)).astype(jnp.bfloat16)
    for t in range(0, length, TILE):
        total = times_rows(high[:, t:t + span], box) + times_rows(low[:, t:t + span], box)
        magnitude = total * (1.0 / (2 * AVG_HALF + 1)) + 1e-5
        normal = (filt[:, t:t + TILE] / magnitude).astype(jnp.bfloat16)
        partners[:, t:t + TILE] = normal[:paired]
        own[:, EDGE + t:EDGE + t + TILE] = normal[paired:]

    factor = float(length) ** -0.5
    half_lags = (LAGS - 1) // 2
    own_wide = own[...]
    results = []
    for g, l0 in enumerate(range(0, LAGS, LAG_GROUP)):
        count = min(LAG_GROUP, LAGS - l0)
        for l in range(count):
            begin = EDGE + half_lags - l0 - l
            toep[(l0 + l) * own_rows:(l0 + l + 1) * own_rows, :] = own_wide[:, begin:begin + length]
        rows = toep[l0 * own_rows:(l0 + count) * own_rows, :]
        sums = (times_rows(rows, partners[...]) * factor).astype(jnp.bfloat16)
        for r in range(ROUNDS):
            part = sums[:, r * block_rows:(r + 1) * block_rows]
            stage[r, l0:l0 + count] = part.reshape(count, own_rows, block_rows)
        result = pltpu.make_async_copy(
            stage.at[:, pl.ds(l0, count)], out_ref.at[:, pl.ds(l0, count)], out_sem.at[g]
        )
        result.start()
        results.append(result)
    for result in results:
        result.wait()


def correlate(everything, plan, taps):
    n_sta, n_tm, block_rows, cols = everything.shape
    length = n_tm * cols
    own_rows = block_rows // n_tm
    rows = ROUNDS * block_rows + own_rows
    wide = length + 2 * EDGE
    groups = -(-LAGS // LAG_GROUP)
    bf16 = jnp.bfloat16
    return pl.pallas_call(
        functools.partial(correlate_kernel, n_tm),
        out_shape=jax.ShapeDtypeStruct((ROUNDS, LAGS, own_rows, block_rows), bf16),
        in_specs=[
            pl.BlockSpec(memory_space=pltpu.SMEM),
            pl.BlockSpec(memory_space=pltpu.VMEM),
            pl.BlockSpec(memory_space=pl.ANY),
        ],
        out_specs=pl.BlockSpec(memory_space=pl.ANY),
        scratch_shapes=[
            pltpu.VMEM((rows, wide), bf16),
            pltpu.VMEM((8, TILE + 2 * EDGE), jnp.float32),
            pltpu.VMEM((rows, length), jnp.float32),
            pltpu.VMEM((rows, wide), bf16),
            pltpu.VMEM((rows, wide), bf16),
            pltpu.VMEM((ROUNDS * block_rows, length), bf16),
            pltpu.VMEM((own_rows, wide), bf16),
            pltpu.VMEM((LAGS * own_rows, length), bf16),
            pltpu.VMEM((ROUNDS, LAGS, own_rows, block_rows), bf16),
            pltpu.SemaphoreType.DMA((ROUNDS + 1, n_tm)),
            pltpu.SemaphoreType.DMA((groups,)),
        ],
        compiler_params=pltpu.CompilerParams(vmem_limit_bytes=60 * 2**20),
        name="correlate_blocks",
    )(plan, taps, everything)


def local(records, filter_taps, plan, station_valid):
    n_sta, n_tm = lax.axis_size("sta"), lax.axis_size("tm")
    everything = gather(records, station_valid[None, :], n_sta, n_tm)
    lagged = correlate(everything, plan, filter_taps[None, :])
    return jnp.transpose(lagged, (0, 2, 1, 3))


def solution(mesh):
    return jax.shard_map(
        local,
        mesh=mesh,
        in_specs=(P("sta", "tm"), P(), P(), P("sta")),
        out_specs=P(None, ("sta", "tm"), None, None),
        check_vma=False,
    )
```

```python
import functools

import jax
import jax.numpy as jnp
from jax import lax
from jax.experimental import pallas as pl
from jax.experimental.pallas import tpu as pltpu
from jax.sharding import PartitionSpec as P

AVG_HALF = 64
LAGS = 101
ROUNDS = 3
TILE = 256
EDGE = 128
LAG_GROUP = 26
MESH = pl.DeviceIdType.MESH


def flipped(index, mask):
    bit = 1
    while bit <= mask:
        if mask & bit:
            index = index + bit - 2 * bit * (lax.div(index, bit) % 2)
        bit *= 2
    return index


def gather_kernel(n_sta, n_tm, valid_ref, rec_ref, all_ref, valid, rec, held, in_sem, keep, z_send, z_recv, send, recv):
    sta = lax.axis_index("sta")
    tm = lax.axis_index("tm")
    bits = n_sta.bit_length() - 1
    outer = list(range(1, bits))

    def chunk_at(position):
        chunk = tm
        for here in range(n_tm):
            near = sorted(range(n_tm), key=lambda there: (abs(there - here), there))
            chunk = jnp.where(tm == here, near[position], chunk)
        return chunk

    chunks = [tm] + [chunk_at(position) for position in range(1, n_tm)]
    inputs = [
        pltpu.make_async_copy(valid_ref, valid, in_sem.at[0]),
        pltpu.make_async_copy(rec_ref, rec, in_sem.at[1]),
    ]
    for copy in inputs:
        copy.start()

    barrier = pltpu.get_barrier_semaphore()
    masks = [1] + list(range(2, n_sta, 2))
    for chunk in chunks[1:]:
        pl.semaphore_signal(barrier, inc=1, device_id=(sta, chunk), device_id_type=MESH)
    for mask in masks:
        pl.semaphore_signal(barrier, inc=1, device_id=(flipped(sta, mask), tm), device_id_type=MESH)

    for copy in inputs:
        copy.wait()
    rows = rec.shape[0]
    row = lax.broadcasted_iota(jnp.int32, (rows, rows), 0)
    col = lax.broadcasted_iota(jnp.int32, (rows, rows), 1)
    alive = jnp.where(row == col, valid[...], 0).astype(jnp.float32).astype(jnp.bfloat16)
    held[0, tm] = jnp.dot(alive, rec[...], preferred_element_type=jnp.float32).astype(jnp.bfloat16)

    pl.semaphore_wait(barrier, len(masks) + n_tm - 1)
    started = []
    kept = []

    def slot(mask, position):
        if mask & 1:
            return all_ref.at[flipped(sta, mask), chunks[position]]
        return held.at[mask // 2, chunks[position]]

    def pass_on(mask, position, jump):
        if jump & 1:
            target = all_ref.at[flipped(sta, mask), chunks[position]]
        else:
            target = held.at[(mask ^ jump) // 2, chunks[position]]
        copy = pltpu.make_async_remote_copy(
            src_ref=slot(mask, position),
            dst_ref=target,
            send_sem=send.at[mask ^ jump, position],
            recv_sem=recv.at[mask ^ jump, position],
            device_id=(flipped(sta, jump), tm),
            device_id_type=MESH,
        )
        copy.start()
        started.append(copy)

    def arrival(sem, mask, position):
        there = slot(mask, position)
        pltpu.make_async_copy(there, there, sem).wait()

    def to_core(mask, position):
        pass_on(mask, position, 1)
        copy = pltpu.make_async_copy(
            held.at[mask // 2, chunks[position]],
            all_ref.at[flipped(sta, mask), chunks[position]],
            keep.at[mask // 2, position],
        )
        copy.start()
        kept.append(copy)

    for position in range(1, n_tm):
        copy = pltpu.make_async_remote_copy(
            src_ref=held.at[0, tm],
            dst_ref=held.at[0, tm],
            send_sem=z_send.at[position],
            recv_sem=z_recv.at[tm],
            device_id=(sta, chunks[position]),
            device_id_type=MESH,
        )
        copy.start()
        started.append(copy)

    def direct(position):
        return position == n_tm - 1 or len(outer) != 2

    def first_bits(position):
        turn = position % 2
        return outer[turn:] + outer[:turn]

    def own_ready(position):
        if position:
            arrival(z_recv.at[chunks[position]], 0, position)
        if direct(position):
            for mask in range(2, n_sta, 2):
                pass_on(0, position, mask)
        else:
            for b in first_bits(position):
                pass_on(0, position, 1 << b)
        to_core(0, position)

    def neighbours(position):
        if not direct(position):
            first, second = first_bits(position)
            arrival(recv.at[1 << first, position], 1 << first, position)
            pass_on(1 << first, position, 1 << second)
            to_core(1 << first, position)
            arrival(recv.at[1 << second, position], 1 << second, position)
            to_core(1 << second, position)

    def far(position):
        for mask in range(2, n_sta, 2):
            if direct(position) or mask == sum(1 << b for b in outer):
                arrival(recv.at[mask, position], mask, position)
                to_core(mask, position)

    for turn in range(n_tm + 2):
        if turn < n_tm:
            own_ready(turn)
        if 1 <= turn <= n_tm:
            neighbours(turn - 1)
        if turn >= 2:
            far(turn - 2)
    for position in range(n_tm):
        for mask in range(1, n_sta, 2):
            arrival(recv.at[mask, position], mask, position)
    for copy in started:
        copy.wait_send()
    for copy in kept:
        copy.wait()


def gather(records, valid, n_sta, n_tm):
    rows, cols = records.shape
    half = max(n_sta // 2, 1)
    return pl.pallas_call(
        functools.partial(gather_kernel, n_sta, n_tm),
        out_shape=jax.ShapeDtypeStruct((n_sta, n_tm, rows, cols), records.dtype),
        in_specs=[pl.BlockSpec(memory_space=pl.ANY)] * 2,
        out_specs=pl.BlockSpec(memory_space=pl.ANY),
        scratch_shapes=[
            pltpu.VMEM(valid.shape, valid.dtype),
            pltpu.VMEM((rows, cols), records.dtype),
            pltpu.VMEM((half, n_tm, rows, cols), records.dtype),
            pltpu.SemaphoreType.DMA((2,)),
            pltpu.SemaphoreType.DMA((half, n_tm)),
            pltpu.SemaphoreType.DMA((n_tm,)),
            pltpu.SemaphoreType.DMA((n_tm,)),
            pltpu.SemaphoreType.DMA((n_sta, n_tm)),
            pltpu.SemaphoreType.DMA((n_sta, n_tm)),
        ],
        compiler_params=pltpu.CompilerParams(
            collective_id=0, has_side_effects=True, vmem_limit_bytes=60 * 2**20
        ),
        name="gather_records",
    )(valid, records)


def times_rows(left, right):
    return lax.dot_general(left, right, (((1,), (1,)), ((), ())), preferred_element_type=jnp.float32)


def correlate_kernel(n_tm, plan_ref, taps_ref, all_ref, out_ref, raw, tapline, filt, high, low, partners, own, toep, stage, in_sem, out_sem):
    block_rows, cols = all_ref.shape[2], all_ref.shape[3]
    length = n_tm * cols
    own_rows = own.shape[0]
    n_taps = taps_ref.shape[1]
    paired = ROUNDS * block_rows
    sta = lax.axis_index("sta")
    copies = []
    for r in range(ROUNDS):
        for c in range(n_tm):
            copies.append(pltpu.make_async_copy(
                all_ref.at[jnp.bitwise_xor(plan_ref[r], sta), c],
                raw.at[pl.ds(r * block_rows, block_rows), pl.ds(EDGE + c * cols, cols)],
                in_sem.at[r, c],
            ))
    first = pl.multiple_of(lax.axis_index("tm") * own_rows, own_rows)
    for c in range(n_tm):
        copies.append(pltpu.make_async_copy(
            all_ref.at[sta, c, pl.ds(first, own_rows), :],
            raw.at[pl.ds(paired, own_rows), pl.ds(EDGE + c * cols, cols)],
            in_sem.at[ROUNDS, c],
        ))
    for copy in copies:
        copy.start()

    for ref in (raw, high, low, own):
        blank = jnp.zeros((ref.shape[0], EDGE), ref.dtype)
        ref[:, :EDGE] = blank
        ref[:, EDGE + length:] = blank
    span = TILE + 2 * EDGE
    tapline[...] = jnp.zeros(tapline.shape, tapline.dtype)
    tapline[0:1, :n_taps] = taps_ref[...]
    line = jnp.broadcast_to(tapline[0:1, :], (TILE, span))
    band = pltpu.roll(line, EDGE - (n_taps - 1) // 2, 1, stride=1, stride_axis=0)
    band_high = band.astype(jnp.bfloat16)
    band_low = (band - band_high.astype(jnp.float32)).astype(jnp.bfloat16)
    ahead = lax.broadcasted_iota(jnp.int32, (TILE, span), 1) - lax.broadcasted_iota(jnp.int32, (TILE, span), 0) - EDGE
    box = jnp.where((ahead >= -AVG_HALF) & (ahead <= AVG_HALF), 1.0, 0.0).astype(jnp.bfloat16)

    for copy in copies:
        copy.wait()
    for t in range(0, length, TILE):
        window = raw[:, t:t + span]
        value = times_rows(window, band_high) + times_rows(window, band_low)
        filt[:, t:t + TILE] = value
        size = jnp.abs(value)
        top = size.astype(jnp.bfloat16)
        high[:, EDGE + t:EDGE + t + TILE] = top
        low[:, EDGE + t:EDGE + t + TILE] = (size - top.astype(jnp.float32)).astype(jnp.bfloat16)
    for t in range(0, length, TILE):
        total = times_rows(high[:, t:t + span], box) + times_rows(low[:, t:t + span], box)
        magnitude = total * (1.0 / (2 * AVG_HALF + 1)) + 1e-5
        normal = (filt[:, t:t + TILE] / magnitude).astype(jnp.bfloat16)
        partners[:, t:t + TILE] = normal[:paired]
        own[:, EDGE + t:EDGE + t + TILE] = normal[paired:]

    factor = float(length) ** -0.5
    half_lags = (LAGS - 1) // 2
    own_wide = own[...]
    results = []
    for g, l0 in enumerate(range(0, LAGS, LAG_GROUP)):
        count = min(LAG_GROUP, LAGS - l0)
        for l in range(count):
            begin = EDGE + half_lags - l0 - l
            toep[(l0 + l) * own_rows:(l0 + l + 1) * own_rows, :] = own_wide[:, begin:begin + length]
        rows = toep[l0 * own_rows:(l0 + count) * own_rows, :]
        sums = (times_rows(rows, partners[...]) * factor).astype(jnp.bfloat16)
        for r in range(ROUNDS):
            part = sums[:, r * block_rows:(r + 1) * block_rows]
            stage[r, l0:l0 + count] = part.reshape(count, own_rows, block_rows)
        result = pltpu.make_async_copy(
            stage.at[:, pl.ds(l0, count)], out_ref.at[:, pl.ds(l0, count)], out_sem.at[g]
        )
        result.start()
        results.append(result)
    for result in results:
        result.wait()


def correlate(everything, plan, taps):
    n_sta, n_tm, block_rows, cols = everything.shape
    length = n_tm * cols
    own_rows = block_rows // n_tm
    rows = ROUNDS * block_rows + own_rows
    wide = length + 2 * EDGE
    groups = -(-LAGS // LAG_GROUP)
    bf16 = jnp.bfloat16
    return pl.pallas_call(
        functools.partial(correlate_kernel, n_tm),
        out_shape=jax.ShapeDtypeStruct((ROUNDS, LAGS, own_rows, block_rows), bf16),
        in_specs=[
            pl.BlockSpec(memory_space=pltpu.SMEM),
            pl.BlockSpec(memory_space=pltpu.VMEM),
            pl.BlockSpec(memory_space=pl.ANY),
        ],
        out_specs=pl.BlockSpec(memory_space=pl.ANY),
        scratch_shapes=[
            pltpu.VMEM((rows, wide), bf16),
            pltpu.VMEM((8, TILE + 2 * EDGE), jnp.float32),
            pltpu.VMEM((rows, length), jnp.float32),
            pltpu.VMEM((rows, wide), bf16),
            pltpu.VMEM((rows, wide), bf16),
            pltpu.VMEM((ROUNDS * block_rows, length), bf16),
            pltpu.VMEM((own_rows, wide), bf16),
            pltpu.VMEM((LAGS * own_rows, length), bf16),
            pltpu.VMEM((ROUNDS, LAGS, own_rows, block_rows), bf16),
            pltpu.SemaphoreType.DMA((ROUNDS + 1, n_tm)),
            pltpu.SemaphoreType.DMA((groups,)),
        ],
        compiler_params=pltpu.CompilerParams(vmem_limit_bytes=60 * 2**20),
        name="correlate_blocks",
    )(plan, taps, everything)


def local(records, filter_taps, plan, station_valid):
    n_sta, n_tm = lax.axis_size("sta"), lax.axis_size("tm")
    everything = gather(records, station_valid[None, :], n_sta, n_tm)
    lagged = correlate(everything, plan, filter_taps[None, :])
    return jnp.transpose(lagged, (0, 2, 1, 3))


def solution(mesh):
    return jax.shard_map(
        local,
        mesh=mesh,
        in_specs=(P("sta", "tm"), P(), P(), P("sta")),
        out_specs=P(None, ("sta", "tm"), None, None),
        check_vma=False,
    )
```

```python
import functools

import jax
import jax.numpy as jnp
from jax import lax
from jax.experimental import pallas as pl
from jax.experimental.pallas import tpu as pltpu
from jax.sharding import PartitionSpec as P

AVG_HALF = 64
LAGS = 101
ROUNDS = 3
TILE = 256
EDGE = 128
LAG_GROUP = 26
MESH = pl.DeviceIdType.MESH


def flipped(index, mask):
    bit = 1
    while bit <= mask:
        if mask & bit:
            index = index + bit - 2 * bit * (lax.div(index, bit) % 2)
        bit *= 2
    return index


def times_rows(left, right):
    return lax.dot_general(left, right, (((1,), (1,)), ((), ())), preferred_element_type=jnp.float32)


def bands(taps_ref, tapline):
    n_taps = taps_ref.shape[1]
    span = TILE + 2 * EDGE
    tapline[...] = jnp.zeros(tapline.shape, tapline.dtype)
    tapline[0:1, :n_taps] = taps_ref[...]
    line = jnp.broadcast_to(tapline[0:1, :], (TILE, span))
    band = pltpu.roll(line, EDGE - (n_taps - 1) // 2, 1, stride=1, stride_axis=0)
    high = band.astype(jnp.bfloat16)
    low = (band - high.astype(jnp.float32)).astype(jnp.bfloat16)
    ahead = lax.broadcasted_iota(jnp.int32, (TILE, span), 1) - lax.broadcasted_iota(jnp.int32, (TILE, span), 0) - EDGE
    box = jnp.where((ahead >= -AVG_HALF) & (ahead <= AVG_HALF), 1.0, 0.0).astype(jnp.bfloat16)
    return high, low, box


def clear_edges(length, *refs):
    for ref in refs:
        blank = jnp.zeros((ref.shape[0], EDGE), ref.dtype)
        ref[:, :EDGE] = blank
        ref[:, EDGE + length:] = blank


def normalise(length, coeffs, raw, filt, size, out, out_edge):
    band_high, band_low, box = coeffs
    span = TILE + 2 * EDGE
    for t in range(0, length, TILE):
        window = raw[:, t:t + span]
        value = times_rows(window, band_high) + times_rows(window, band_low)
        filt[:, t:t + TILE] = value
        size[:, EDGE + t:EDGE + t + TILE] = jnp.abs(value).astype(jnp.bfloat16)
    for t in range(0, length, TILE):
        magnitude = times_rows(size[:, t:t + span], box) * (1.0 / (2 * AVG_HALF + 1)) + 1e-5
        out[:, out_edge + t:out_edge + t + TILE] = (filt[:, t:t + TILE] / magnitude).astype(jnp.bfloat16)


def lag_groups():
    return [(l0, min(LAG_GROUP, LAGS - l0)) for l0 in range(0, LAGS, LAG_GROUP)]


def gather_kernel(
    n_sta, n_tm, taps_ref, valid_ref, rec_ref, all_ref, toep_ref,
    valid, rec, held, tapline, raw, filt, size, own, toep,
    in_sem, keep, z_send, z_recv, send, recv, toep_sem,
):
    sta = lax.axis_index("sta")
    tm = lax.axis_index("tm")
    bits = n_sta.bit_length() - 1
    outer = list(range(1, bits))

    def chunk_at(position):
        chunk = tm
        for here in range(n_tm):
            near = sorted(range(n_tm), key=lambda there: (abs(there - here), there))
            chunk = jnp.where(tm == here, near[position], chunk)
        return chunk

    chunks = [tm] + [chunk_at(position) for position in range(1, n_tm)]
    inputs = [
        pltpu.make_async_copy(valid_ref, valid, in_sem.at[0]),
        pltpu.make_async_copy(rec_ref, rec, in_sem.at[1]),
    ]
    for copy in inputs:
        copy.start()

    barrier = pltpu.get_barrier_semaphore()
    masks = [1] + list(range(2, n_sta, 2))
    for chunk in chunks[1:]:
        pl.semaphore_signal(barrier, inc=1, device_id=(sta, chunk), device_id_type=MESH)
    for mask in masks:
        pl.semaphore_signal(barrier, inc=1, device_id=(flipped(sta, mask), tm), device_id_type=MESH)

    for copy in inputs:
        copy.wait()
    rows = rec.shape[0]
    row = lax.broadcasted_iota(jnp.int32, (rows, rows), 0)
    col = lax.broadcasted_iota(jnp.int32, (rows, rows), 1)
    alive = jnp.where(row == col, valid[...], 0).astype(jnp.float32).astype(jnp.bfloat16)
    held[0, tm] = jnp.dot(alive, rec[...], preferred_element_type=jnp.float32).astype(jnp.bfloat16)

    own_rows, cols = own.shape[0], rec.shape[1]
    length = n_tm * cols
    clear_edges(length, raw, size, own)
    coeffs = bands(taps_ref, tapline)

    pl.semaphore_wait(barrier, len(masks) + n_tm - 1)
    started = []
    kept = []

    def slot(mask, position):
        if mask & 1:
            return all_ref.at[flipped(sta, mask), chunks[position]]
        return held.at[mask // 2, chunks[position]]

    def pass_on(mask, position, jump):
        if jump & 1:
            target = all_ref.at[flipped(sta, mask), chunks[position]]
        else:
            target = held.at[(mask ^ jump) // 2, chunks[position]]
        copy = pltpu.make_async_remote_copy(
            src_ref=slot(mask, position),
            dst_ref=target,
            send_sem=send.at[mask ^ jump, position],
            recv_sem=recv.at[mask ^ jump, position],
            device_id=(flipped(sta, jump), tm),
            device_id_type=MESH,
        )
        copy.start()
        started.append(copy)

    def arrival(sem, mask, position):
        there = slot(mask, position)
        pltpu.make_async_copy(there, there, sem).wait()

    def to_core(mask, position):
        pass_on(mask, position, 1)
        copy = pltpu.make_async_copy(
            held.at[mask // 2, chunks[position]],
            all_ref.at[flipped(sta, mask), chunks[position]],
            keep.at[mask // 2, position],
        )
        copy.start()
        kept.append(copy)

    for position in range(1, n_tm):
        copy = pltpu.make_async_remote_copy(
            src_ref=held.at[0, tm],
            dst_ref=held.at[0, tm],
            send_sem=z_send.at[position],
            recv_sem=z_recv.at[tm],
            device_id=(sta, chunks[position]),
            device_id_type=MESH,
        )
        copy.start()
        started.append(copy)

    def direct(position):
        return position == n_tm - 1 or len(outer) != 2

    def first_bits(position):
        turn = position % 2
        return outer[turn:] + outer[:turn]

    def own_ready(position):
        if position:
            arrival(z_recv.at[chunks[position]], 0, position)
        if direct(position):
            for mask in range(2, n_sta, 2):
                pass_on(0, position, mask)
        else:
            for b in first_bits(position):
                pass_on(0, position, 1 << b)
        to_core(0, position)

    def neighbours(position):
        if not direct(position):
            first, second = first_bits(position)
            arrival(recv.at[1 << first, position], 1 << first, position)
            pass_on(1 << first, position, 1 << second)
            to_core(1 << first, position)
            arrival(recv.at[1 << second, position], 1 << second, position)
            to_core(1 << second, position)

    def far(position):
        for mask in range(2, n_sta, 2):
            if direct(position) or mask == sum(1 << b for b in outer):
                arrival(recv.at[mask, position], mask, position)
                to_core(mask, position)

    def normalise_own():
        first = pl.multiple_of(tm * own_rows, own_rows)
        for c in range(n_tm):
            raw[:, EDGE + c * cols:EDGE + (c + 1) * cols] = held[0, c, pl.ds(first, own_rows), :]
        normalise(length, coeffs, raw, filt, size, own, EDGE)

    def lagged_rows(group):
        l0, count = lag_groups()[group]
        own_wide = own[...]
        for l in range(l0, l0 + count):
            begin = EDGE + (LAGS - 1) // 2 - l
            toep[l * own_rows:(l + 1) * own_rows, :] = own_wide[:, begin:begin + length]
        part = pl.ds(l0 * own_rows, count * own_rows)
        copy = pltpu.make_async_copy(toep.at[part], toep_ref.at[part], toep_sem.at[group])
        copy.start()
        kept.append(copy)

    work = [normalise_own] + [functools.partial(lagged_rows, g) for g in range(len(lag_groups()))]
    for turn in range(n_tm + 2):
        if turn < n_tm:
            own_ready(turn)
        if 1 <= turn <= n_tm:
            neighbours(turn - 1)
        if turn >= 2:
            far(turn - 2)
        if turn >= n_tm - 1:
            work.pop(0)()
    for step in work:
        step()
    for position in range(n_tm):
        for mask in range(1, n_sta, 2):
            arrival(recv.at[mask, position], mask, position)
    for copy in started:
        copy.wait_send()
    for copy in kept:
        copy.wait()


def gather(records, valid, taps, n_sta, n_tm):
    rows, cols = records.shape
    own_rows, length = rows // n_tm, n_tm * cols
    wide = length + 2 * EDGE
    bf16 = jnp.bfloat16
    half = max(n_sta // 2, 1)
    return pl.pallas_call(
        functools.partial(gather_kernel, n_sta, n_tm),
        out_shape=[
            jax.ShapeDtypeStruct((n_sta, n_tm, rows, cols), records.dtype),
            jax.ShapeDtypeStruct((LAGS * own_rows, length), bf16),
        ],
        in_specs=[pl.BlockSpec(memory_space=pltpu.VMEM)] + [pl.BlockSpec(memory_space=pl.ANY)] * 2,
        out_specs=[pl.BlockSpec(memory_space=pl.ANY)] * 2,
        scratch_shapes=[
            pltpu.VMEM(valid.shape, valid.dtype),
            pltpu.VMEM((rows, cols), records.dtype),
            pltpu.VMEM((half, n_tm, rows, cols), records.dtype),
            pltpu.VMEM((8, TILE + 2 * EDGE), jnp.float32),
            pltpu.VMEM((own_rows, wide), bf16),
            pltpu.VMEM((own_rows, length), jnp.float32),
            pltpu.VMEM((own_rows, wide), bf16),
            pltpu.VMEM((own_rows, wide), bf16),
            pltpu.VMEM((LAGS * own_rows, length), bf16),
            pltpu.SemaphoreType.DMA((2,)),
            pltpu.SemaphoreType.DMA((half, n_tm)),
            pltpu.SemaphoreType.DMA((n_tm,)),
            pltpu.SemaphoreType.DMA((n_tm,)),
            pltpu.SemaphoreType.DMA((n_sta, n_tm)),
            pltpu.SemaphoreType.DMA((n_sta, n_tm)),
            pltpu.SemaphoreType.DMA((len(lag_groups()),)),
        ],
        compiler_params=pltpu.CompilerParams(
            collective_id=0, has_side_effects=True, vmem_limit_bytes=60 * 2**20
        ),
        name="gather_records",
    )(taps, valid, records)


def correlate_kernel(n_tm, plan_ref, taps_ref, all_ref, toep_ref, out_ref, raw, tapline, filt, size, partners, toep, stage, in_sem, toep_sem, out_sem):
    block_rows, cols = all_ref.shape[2], all_ref.shape[3]
    length = n_tm * cols
    own_rows = toep.shape[0] // LAGS
    sta = lax.axis_index("sta")
    copies = []
    for r in range(ROUNDS):
        for c in range(n_tm):
            copies.append(pltpu.make_async_copy(
                all_ref.at[jnp.bitwise_xor(plan_ref[r], sta), c],
                raw.at[pl.ds(r * block_rows, block_rows), pl.ds(EDGE + c * cols, cols)],
                in_sem.at[r, c],
            ))
    toep_copies = []
    for g, (l0, count) in enumerate(lag_groups()):
        part = pl.ds(l0 * own_rows, count * own_rows)
        toep_copies.append(pltpu.make_async_copy(toep_ref.at[part], toep.at[part], toep_sem.at[g]))
    for copy in copies + toep_copies:
        copy.start()

    clear_edges(length, raw, size)
    coeffs = bands(taps_ref, tapline)
    for copy in copies:
        copy.wait()
    normalise(length, coeffs, raw, filt, size, partners, 0)

    factor = float(length) ** -0.5
    results = []
    for g, (l0, count) in enumerate(lag_groups()):
        toep_copies[g].wait()
        rows = toep[l0 * own_rows:(l0 + count) * own_rows, :]
        sums = (times_rows(rows, partners[...]) * factor).astype(jnp.bfloat16)
        for r in range(ROUNDS):
            part = sums[:, r * block_rows:(r + 1) * block_rows]
            stage[r, l0:l0 + count] = part.reshape(count, own_rows, block_rows)
        result = pltpu.make_async_copy(
            stage.at[:, pl.ds(l0, count)], out_ref.at[:, pl.ds(l0, count)], out_sem.at[g]
        )
        result.start()
        results.append(result)
    for result in results:
        result.wait()


def correlate(everything, toep, plan, taps):
    n_sta, n_tm, block_rows, cols = everything.shape
    length = n_tm * cols
    own_rows = block_rows // n_tm
    rows = ROUNDS * block_rows
    wide = length + 2 * EDGE
    bf16 = jnp.bfloat16
    return pl.pallas_call(
        functools.partial(correlate_kernel, n_tm),
        out_shape=jax.ShapeDtypeStruct((ROUNDS, LAGS, own_rows, block_rows), bf16),
        in_specs=[
            pl.BlockSpec(memory_space=pltpu.SMEM),
            pl.BlockSpec(memory_space=pltpu.VMEM),
            pl.BlockSpec(memory_space=pl.ANY),
            pl.BlockSpec(memory_space=pl.ANY),
        ],
        out_specs=pl.BlockSpec(memory_space=pl.ANY),
        scratch_shapes=[
            pltpu.VMEM((rows, wide), bf16),
            pltpu.VMEM((8, TILE + 2 * EDGE), jnp.float32),
            pltpu.VMEM((rows, length), jnp.float32),
            pltpu.VMEM((rows, wide), bf16),
            pltpu.VMEM((rows, length), bf16),
            pltpu.VMEM(toep.shape, bf16),
            pltpu.VMEM((ROUNDS, LAGS, own_rows, block_rows), bf16),
            pltpu.SemaphoreType.DMA((ROUNDS, n_tm)),
            pltpu.SemaphoreType.DMA((len(lag_groups()),)),
            pltpu.SemaphoreType.DMA((len(lag_groups()),)),
        ],
        compiler_params=pltpu.CompilerParams(vmem_limit_bytes=60 * 2**20),
        name="correlate_blocks",
    )(plan, taps, everything, toep)


def local(records, filter_taps, plan, station_valid):
    n_sta, n_tm = lax.axis_size("sta"), lax.axis_size("tm")
    taps = filter_taps[None, :]
    everything, toep = gather(records, station_valid[None, :], taps, n_sta, n_tm)
    lagged = correlate(everything, toep, plan, taps)
    return jnp.transpose(lagged, (0, 2, 1, 3))


def solution(mesh):
    return jax.shard_map(
        local,
        mesh=mesh,
        in_specs=(P("sta", "tm"), P(), P(), P("sta")),
        out_specs=P(None, ("sta", "tm"), None, None),
        check_vma=False,
    )
```

```python
import functools

import jax
import jax.numpy as jnp
from jax import lax
from jax.experimental import pallas as pl
from jax.experimental.pallas import tpu as pltpu
from jax.sharding import PartitionSpec as P

AVG_HALF = 64
LAGS = 101
ROUNDS = 3
TILE = 256
EDGE = 128
LAG_GROUP = 26
MESH = pl.DeviceIdType.MESH


def flipped(index, mask):
    bit = 1
    while bit <= mask:
        if mask & bit:
            index = index + bit - 2 * bit * (lax.div(index, bit) % 2)
        bit *= 2
    return index


def times_rows(left, right):
    return lax.dot_general(left, right, (((1,), (1,)), ((), ())), preferred_element_type=jnp.float32)


def bands(taps_ref, tapline):
    n_taps = taps_ref.shape[1]
    span = TILE + 2 * EDGE
    tapline[...] = jnp.zeros(tapline.shape, tapline.dtype)
    tapline[0:1, :n_taps] = taps_ref[...]
    line = jnp.broadcast_to(tapline[0:1, :], (TILE, span))
    band = pltpu.roll(line, EDGE - (n_taps - 1) // 2, 1, stride=1, stride_axis=0)
    high = band.astype(jnp.bfloat16)
    low = (band - high.astype(jnp.float32)).astype(jnp.bfloat16)
    ahead = lax.broadcasted_iota(jnp.int32, (TILE, span), 1) - lax.broadcasted_iota(jnp.int32, (TILE, span), 0) - EDGE
    box = jnp.where((ahead >= -AVG_HALF) & (ahead <= AVG_HALF), 1.0, 0.0).astype(jnp.bfloat16)
    return high, low, box


def clear_edges(length, *refs):
    for ref in refs:
        blank = jnp.zeros((ref.shape[0], EDGE), ref.dtype)
        ref[:, :EDGE] = blank
        ref[:, EDGE + length:] = blank


def normalise(length, coeffs, raw, filt, size, rest, out, out_edge):
    band_high, band_low, box = coeffs
    span = TILE + 2 * EDGE
    for t in range(0, length, TILE):
        window = raw[:, t:t + span]
        value = times_rows(window, band_high) + times_rows(window, band_low)
        filt[:, t:t + TILE] = value
        whole = jnp.abs(value)
        part = whole.astype(jnp.bfloat16)
        size[:, EDGE + t:EDGE + t + TILE] = part
        rest[:, EDGE + t:EDGE + t + TILE] = (whole - part.astype(jnp.float32)).astype(jnp.bfloat16)
    for t in range(0, length, TILE):
        total = times_rows(size[:, t:t + span], box) + times_rows(rest[:, t:t + span], box)
        magnitude = total * (1.0 / (2 * AVG_HALF + 1)) + 1e-5
        out[:, out_edge + t:out_edge + t + TILE] = (filt[:, t:t + TILE] / magnitude).astype(jnp.bfloat16)


def lag_groups():
    return [(l0, min(LAG_GROUP, LAGS - l0)) for l0 in range(0, LAGS, LAG_GROUP)]


def gather_kernel(
    n_sta, n_tm, taps_ref, valid_ref, rec_ref, all_ref, own_ref,
    taps, valid, rec, held, tapline, raw, filt, size, rest, own,
    in_sem, keep, z_send, z_recv, send, recv, own_sem,
):
    sta = lax.axis_index("sta")
    tm = lax.axis_index("tm")
    bits = n_sta.bit_length() - 1
    outer = list(range(1, bits))

    def chunk_at(position):
        chunk = tm
        for here in range(n_tm):
            near = sorted(range(n_tm), key=lambda there: (abs(there - here), there))
            chunk = jnp.where(tm == here, near[position], chunk)
        return chunk

    chunks = [tm] + [chunk_at(position) for position in range(1, n_tm)]
    inputs = [
        pltpu.make_async_copy(valid_ref, valid, in_sem.at[0]),
        pltpu.make_async_copy(rec_ref, rec, in_sem.at[1]),
        pltpu.make_async_copy(taps_ref, taps, in_sem.at[2]),
    ]
    for copy in inputs:
        copy.start()

    barrier = pltpu.get_barrier_semaphore()
    masks = [1] + list(range(2, n_sta, 2))
    for chunk in chunks[1:]:
        pl.semaphore_signal(barrier, inc=1, device_id=(sta, chunk), device_id_type=MESH)
    for mask in masks:
        pl.semaphore_signal(barrier, inc=1, device_id=(flipped(sta, mask), tm), device_id_type=MESH)

    for copy in inputs:
        copy.wait()
    rows = rec.shape[0]
    row = lax.broadcasted_iota(jnp.int32, (rows, rows), 0)
    col = lax.broadcasted_iota(jnp.int32, (rows, rows), 1)
    alive = jnp.where(row == col, valid[...], 0).astype(jnp.float32).astype(jnp.bfloat16)
    held[0, tm] = jnp.dot(alive, rec[...], preferred_element_type=jnp.float32).astype(jnp.bfloat16)

    own_rows, cols = own.shape[0], rec.shape[1]
    length = n_tm * cols
    clear_edges(length, raw, size, rest, own)

    pl.semaphore_wait(barrier, len(masks) + n_tm - 1)
    started = []
    kept = []

    def slot(mask, position):
        if mask & 1:
            return all_ref.at[flipped(sta, mask), chunks[position]]
        return held.at[mask // 2, chunks[position]]

    def pass_on(mask, position, jump):
        if jump & 1:
            target = all_ref.at[flipped(sta, mask), chunks[position]]
        else:
            target = held.at[(mask ^ jump) // 2, chunks[position]]
        copy = pltpu.make_async_remote_copy(
            src_ref=slot(mask, position),
            dst_ref=target,
            send_sem=send.at[mask ^ jump, position],
            recv_sem=recv.at[mask ^ jump, position],
            device_id=(flipped(sta, jump), tm),
            device_id_type=MESH,
        )
        copy.start()
        started.append(copy)

    def arrival(sem, mask, position):
        there = slot(mask, position)
        pltpu.make_async_copy(there, there, sem).wait()

    def to_core(mask, position):
        pass_on(mask, position, 1)
        copy = pltpu.make_async_copy(
            held.at[mask // 2, chunks[position]],
            all_ref.at[flipped(sta, mask), chunks[position]],
            keep.at[mask // 2, position],
        )
        copy.start()
        kept.append(copy)

    for position in range(1, n_tm):
        copy = pltpu.make_async_remote_copy(
            src_ref=held.at[0, tm],
            dst_ref=held.at[0, tm],
            send_sem=z_send.at[position],
            recv_sem=z_recv.at[tm],
            device_id=(sta, chunks[position]),
            device_id_type=MESH,
        )
        copy.start()
        started.append(copy)

    def direct(position):
        return position == n_tm - 1 or len(outer) != 2

    def first_bits(position):
        turn = position % 2
        return outer[turn:] + outer[:turn]

    def own_ready(position):
        if position:
            arrival(z_recv.at[chunks[position]], 0, position)
        if direct(position):
            for mask in range(2, n_sta, 2):
                pass_on(0, position, mask)
        else:
            for b in first_bits(position):
                pass_on(0, position, 1 << b)
        to_core(0, position)

    def neighbours(position):
        if not direct(position):
            first, second = first_bits(position)
            arrival(recv.at[1 << first, position], 1 << first, position)
            pass_on(1 << first, position, 1 << second)
            to_core(1 << first, position)
            arrival(recv.at[1 << second, position], 1 << second, position)
            to_core(1 << second, position)

    def far(position):
        for mask in range(2, n_sta, 2):
            if direct(position) or mask == sum(1 << b for b in outer):
                arrival(recv.at[mask, position], mask, position)
                to_core(mask, position)

    for turn in range(n_tm + 2):
        if turn < n_tm:
            own_ready(turn)
        if 1 <= turn <= n_tm:
            neighbours(turn - 1)
        if turn >= 2:
            far(turn - 2)

    first = pl.multiple_of(tm * own_rows, own_rows)
    for c in range(n_tm):
        raw[:, EDGE + c * cols:EDGE + (c + 1) * cols] = held[0, c, pl.ds(first, own_rows), :]
    normalise(length, bands(taps, tapline), raw, filt, size, rest, own, EDGE)
    own_copy = pltpu.make_async_copy(own, own_ref, own_sem)
    own_copy.start()
    kept.append(own_copy)
    for position in range(n_tm):
        for mask in range(1, n_sta, 2):
            arrival(recv.at[mask, position], mask, position)
    for copy in started:
        copy.wait_send()
    for copy in kept:
        copy.wait()


def gather(records, valid, taps, n_sta, n_tm):
    rows, cols = records.shape
    own_rows, length = rows // n_tm, n_tm * cols
    wide = length + 2 * EDGE
    bf16 = jnp.bfloat16
    half = max(n_sta // 2, 1)
    return pl.pallas_call(
        functools.partial(gather_kernel, n_sta, n_tm),
        out_shape=[
            jax.ShapeDtypeStruct((n_sta, n_tm, rows, cols), records.dtype),
            jax.ShapeDtypeStruct((own_rows, wide), bf16),
        ],
        in_specs=[pl.BlockSpec(memory_space=pltpu.HBM)] * 3,
        out_specs=[pl.BlockSpec(memory_space=pl.ANY)] * 2,
        scratch_shapes=[
            pltpu.VMEM(taps.shape, taps.dtype),
            pltpu.VMEM(valid.shape, valid.dtype),
            pltpu.VMEM((rows, cols), records.dtype),
            pltpu.VMEM((half, n_tm, rows, cols), records.dtype),
            pltpu.VMEM((8, TILE + 2 * EDGE), jnp.float32),
            pltpu.VMEM((own_rows, wide), bf16),
            pltpu.VMEM((own_rows, length), jnp.float32),
            pltpu.VMEM((own_rows, wide), bf16),
            pltpu.VMEM((own_rows, wide), bf16),
            pltpu.VMEM((own_rows, wide), bf16),
            pltpu.SemaphoreType.DMA((3,)),
            pltpu.SemaphoreType.DMA((half, n_tm)),
            pltpu.SemaphoreType.DMA((n_tm,)),
            pltpu.SemaphoreType.DMA((n_tm,)),
            pltpu.SemaphoreType.DMA((n_sta, n_tm)),
            pltpu.SemaphoreType.DMA((n_sta, n_tm)),
            pltpu.SemaphoreType.DMA,
        ],
        compiler_params=pltpu.CompilerParams(
            collective_id=0,
            has_side_effects=True,
            vmem_limit_bytes=60 * 2**20,
        ),
        name="gather_records",
    )(taps, valid, records)


def correlate_kernel(n_tm, plan_ref, taps_ref, all_ref, own_ref, out_ref, taps, own, raw, tapline, filt, size, rest, partners, toep, stage, small_sem, in_sem, out_sem):
    block_rows, cols = all_ref.shape[2], all_ref.shape[3]
    length = n_tm * cols
    own_rows = own.shape[0]
    sta = lax.axis_index("sta")
    copies = []
    for r in range(ROUNDS):
        for c in range(n_tm):
            copies.append(pltpu.make_async_copy(
                all_ref.at[jnp.bitwise_xor(plan_ref[r], sta), c],
                raw.at[pl.ds(r * block_rows, block_rows), pl.ds(EDGE + c * cols, cols)],
                in_sem.at[r, c],
            ))
    small = [
        pltpu.make_async_copy(own_ref, own, small_sem.at[0]),
        pltpu.make_async_copy(taps_ref, taps, small_sem.at[1]),
    ]
    for copy in small + copies:
        copy.start()

    def lagged_rows(group):
        l0, count = lag_groups()[group]
        own_wide = own[...]
        for l in range(l0, l0 + count):
            begin = EDGE + (LAGS - 1) // 2 - l
            toep[l * own_rows:(l + 1) * own_rows, :] = own_wide[:, begin:begin + length]

    groups = len(lag_groups())
    early = groups // 2
    clear_edges(length, raw, size, rest)
    for copy in small:
        copy.wait()
    coeffs = bands(taps, tapline)
    for g in range(early):
        lagged_rows(g)
    for copy in copies:
        copy.wait()
    normalise(length, coeffs, raw, filt, size, rest, partners, 0)

    factor = float(length) ** -0.5
    results = []
    for g, (l0, count) in enumerate(lag_groups()):
        if g + early < groups:
            lagged_rows(g + early)
        rows = toep[l0 * own_rows:(l0 + count) * own_rows, :]
        sums = (times_rows(rows, partners[...]) * factor).astype(jnp.bfloat16)
        for r in range(ROUNDS):
            part = sums[:, r * block_rows:(r + 1) * block_rows]
            stage[r, l0:l0 + count] = part.reshape(count, own_rows, block_rows)
        result = pltpu.make_async_copy(
            stage.at[:, pl.ds(l0, count)], out_ref.at[:, pl.ds(l0, count)], out_sem.at[g]
        )
        result.start()
        results.append(result)
    for result in results:
        result.wait()


def correlate(everything, own, plan, taps):
    n_sta, n_tm, block_rows, cols = everything.shape
    length = n_tm * cols
    own_rows = block_rows // n_tm
    rows = ROUNDS * block_rows
    wide = length + 2 * EDGE
    bf16 = jnp.bfloat16
    return pl.pallas_call(
        functools.partial(correlate_kernel, n_tm),
        out_shape=jax.ShapeDtypeStruct((ROUNDS, LAGS, own_rows, block_rows), bf16),
        in_specs=[
            pl.BlockSpec(memory_space=pltpu.SMEM),
            pl.BlockSpec(memory_space=pltpu.HBM),
            pl.BlockSpec(memory_space=pl.ANY),
            pl.BlockSpec(memory_space=pl.ANY),
        ],
        out_specs=pl.BlockSpec(memory_space=pl.ANY),
        scratch_shapes=[
            pltpu.VMEM(taps.shape, taps.dtype),
            pltpu.VMEM(own.shape, bf16),
            pltpu.VMEM((rows, wide), bf16),
            pltpu.VMEM((8, TILE + 2 * EDGE), jnp.float32),
            pltpu.VMEM((rows, length), jnp.float32),
            pltpu.VMEM((rows, wide), bf16),
            pltpu.VMEM((rows, wide), bf16),
            pltpu.VMEM((rows, length), bf16),
            pltpu.VMEM((LAGS * own_rows, length), bf16),
            pltpu.VMEM((ROUNDS, LAGS, own_rows, block_rows), bf16),
            pltpu.SemaphoreType.DMA((2,)),
            pltpu.SemaphoreType.DMA((ROUNDS, n_tm)),
            pltpu.SemaphoreType.DMA((len(lag_groups()),)),
        ],
        compiler_params=pltpu.CompilerParams(vmem_limit_bytes=60 * 2**20),
        name="correlate_blocks",
    )(plan, taps, everything, own)


def local(records, filter_taps, plan, station_valid):
    n_sta, n_tm = lax.axis_size("sta"), lax.axis_size("tm")
    taps = filter_taps[None, :]
    everything, own = gather(records, station_valid[None, :], taps, n_sta, n_tm)
    lagged = correlate(everything, own, plan, taps)
    return jnp.transpose(lagged, (0, 2, 1, 3))


def solution(mesh):
    return jax.shard_map(
        local,
        mesh=mesh,
        in_specs=(P("sta", "tm"), P(), P(), P("sta")),
        out_specs=P(None, ("sta", "tm"), None, None),
        check_vma=False,
    )
```

```python
import functools

import jax
import jax.numpy as jnp
from jax import lax
from jax.experimental import pallas as pl
from jax.experimental.pallas import tpu as pltpu
from jax.sharding import PartitionSpec as P

AVG_HALF = 64
LAGS = 101
ROUNDS = 3
TILE = 256
EDGE = 128
BASE_GROUP = 13
MESH = pl.DeviceIdType.MESH


def flipped(index, mask):
    bit = 1
    while bit <= mask:
        if mask & bit:
            index = index + bit - 2 * bit * (lax.div(index, bit) % 2)
        bit *= 2
    return index


def gather_kernel(n_sta, n_tm, valid_ref, rec_ref, all_ref, valid, rec, held, in_sem, keep, z_send, z_recv, send, recv):
    sta = lax.axis_index("sta")
    tm = lax.axis_index("tm")
    bits = n_sta.bit_length() - 1
    outer = list(range(1, bits))

    def chunk_at(position):
        chunk = tm
        for here in range(n_tm):
            near = sorted(range(n_tm), key=lambda there: (abs(there - here), there))
            chunk = jnp.where(tm == here, near[position], chunk)
        return chunk

    chunks = [tm] + [chunk_at(position) for position in range(1, n_tm)]
    inputs = [
        pltpu.make_async_copy(valid_ref, valid, in_sem.at[0]),
        pltpu.make_async_copy(rec_ref, rec, in_sem.at[1]),
    ]
    for copy in inputs:
        copy.start()

    barrier = pltpu.get_barrier_semaphore()
    masks = [1] + list(range(2, n_sta, 2))
    for chunk in chunks[1:]:
        pl.semaphore_signal(barrier, inc=1, device_id=(sta, chunk), device_id_type=MESH)
    for mask in masks:
        pl.semaphore_signal(barrier, inc=1, device_id=(flipped(sta, mask), tm), device_id_type=MESH)

    for copy in inputs:
        copy.wait()
    rows = rec.shape[0]
    row = lax.broadcasted_iota(jnp.int32, (rows, rows), 0)
    col = lax.broadcasted_iota(jnp.int32, (rows, rows), 1)
    alive = jnp.where(row == col, valid[...], 0).astype(jnp.float32).astype(jnp.bfloat16)
    held[0, tm] = jnp.dot(alive, rec[...], preferred_element_type=jnp.float32).astype(jnp.bfloat16)

    pl.semaphore_wait(barrier, len(masks) + n_tm - 1)
    started = []
    kept = []

    def slot(mask, position):
        if mask & 1:
            return all_ref.at[flipped(sta, mask), chunks[position]]
        return held.at[mask // 2, chunks[position]]

    def pass_on(mask, position, jump):
        if jump & 1:
            target = all_ref.at[flipped(sta, mask), chunks[position]]
        else:
            target = held.at[(mask ^ jump) // 2, chunks[position]]
        copy = pltpu.make_async_remote_copy(
            src_ref=slot(mask, position),
            dst_ref=target,
            send_sem=send.at[mask ^ jump, position],
            recv_sem=recv.at[mask ^ jump, position],
            device_id=(flipped(sta, jump), tm),
            device_id_type=MESH,
        )
        copy.start()
        started.append(copy)

    def arrival(sem, mask, position):
        there = slot(mask, position)
        pltpu.make_async_copy(there, there, sem).wait()

    def to_core(mask, position):
        pass_on(mask, position, 1)
        copy = pltpu.make_async_copy(
            held.at[mask // 2, chunks[position]],
            all_ref.at[flipped(sta, mask), chunks[position]],
            keep.at[mask // 2, position],
        )
        copy.start()
        kept.append(copy)

    for position in range(1, n_tm):
        copy = pltpu.make_async_remote_copy(
            src_ref=held.at[0, tm],
            dst_ref=held.at[0, tm],
            send_sem=z_send.at[position],
            recv_sem=z_recv.at[tm],
            device_id=(sta, chunks[position]),
            device_id_type=MESH,
        )
        copy.start()
        started.append(copy)

    def direct(position):
        return position == n_tm - 1 or len(outer) != 2

    def first_bits(position):
        turn = position % 2
        return outer[turn:] + outer[:turn]

    def own_ready(position):
        if position:
            arrival(z_recv.at[chunks[position]], 0, position)
        if direct(position):
            for mask in range(2, n_sta, 2):
                pass_on(0, position, mask)
        else:
            for b in first_bits(position):
                pass_on(0, position, 1 << b)
        to_core(0, position)

    def neighbours(position):
        if not direct(position):
            first, second = first_bits(position)
            arrival(recv.at[1 << first, position], 1 << first, position)
            pass_on(1 << first, position, 1 << second)
            to_core(1 << first, position)
            arrival(recv.at[1 << second, position], 1 << second, position)
            to_core(1 << second, position)

    def far(position):
        for mask in range(2, n_sta, 2):
            if direct(position) or mask == sum(1 << b for b in outer):
                arrival(recv.at[mask, position], mask, position)
                to_core(mask, position)

    for turn in range(n_tm + 2):
        if turn < n_tm:
            own_ready(turn)
        if 1 <= turn <= n_tm:
            neighbours(turn - 1)
        if turn >= 2:
            far(turn - 2)
    for position in range(n_tm):
        for mask in range(1, n_sta, 2):
            arrival(recv.at[mask, position], mask, position)
    for copy in started:
        copy.wait_send()
    for copy in kept:
        copy.wait()


def gather(records, valid, n_sta, n_tm):
    rows, cols = records.shape
    half = max(n_sta // 2, 1)
    return pl.pallas_call(
        functools.partial(gather_kernel, n_sta, n_tm),
        out_shape=jax.ShapeDtypeStruct((n_sta, n_tm, rows, cols), records.dtype),
        in_specs=[pl.BlockSpec(memory_space=pl.ANY)] * 2,
        out_specs=pl.BlockSpec(memory_space=pl.ANY),
        scratch_shapes=[
            pltpu.VMEM(valid.shape, valid.dtype),
            pltpu.VMEM((rows, cols), records.dtype),
            pltpu.VMEM((half, n_tm, rows, cols), records.dtype),
            pltpu.SemaphoreType.DMA((2,)),
            pltpu.SemaphoreType.DMA((half, n_tm)),
            pltpu.SemaphoreType.DMA((n_tm,)),
            pltpu.SemaphoreType.DMA((n_tm,)),
            pltpu.SemaphoreType.DMA((n_sta, n_tm)),
            pltpu.SemaphoreType.DMA((n_sta, n_tm)),
        ],
        compiler_params=pltpu.CompilerParams(
            collective_id=0, has_side_effects=True, vmem_limit_bytes=60 * 2**20
        ),
        name="gather_records",
    )(valid, records)


def times_rows(left, right):
    return lax.dot_general(left, right, (((1,), (1,)), ((), ())), preferred_element_type=jnp.float32)


def base_groups():
    half = (LAGS - 1) // 2
    groups = []
    for bases in (list(range(half % 2, half + 1, 2)), list(range(half + 1, LAGS, 2))):
        groups += [bases[i:i + BASE_GROUP] for i in range(0, len(bases), BASE_GROUP)]
    return groups


def correlate_kernel(n_tm, plan_ref, taps_ref, all_ref, out_ref, raw, tapline, filt, high, low, partners, toep, stage, in_sem, out_sem):
    block_rows, cols = all_ref.shape[2], all_ref.shape[3]
    length = n_tm * cols
    own_rows = block_rows // n_tm
    n_taps = taps_ref.shape[1]
    paired = ROUNDS * block_rows
    sta = lax.axis_index("sta")
    copies = []
    for r in range(ROUNDS):
        for c in range(n_tm):
            copies.append(pltpu.make_async_copy(
                all_ref.at[jnp.bitwise_xor(plan_ref[r], sta), c],
                raw.at[pl.ds(r * block_rows, block_rows), pl.ds(EDGE + c * cols, cols)],
                in_sem.at[r, c],
            ))
    first = pl.multiple_of(lax.axis_index("tm") * own_rows, own_rows)
    for c in range(n_tm):
        copies.append(pltpu.make_async_copy(
            all_ref.at[sta, c, pl.ds(first, own_rows), :],
            raw.at[pl.ds(paired, own_rows), pl.ds(EDGE + c * cols, cols)],
            in_sem.at[ROUNDS, c],
        ))
    for copy in copies:
        copy.start()

    for ref in (raw, high, low):
        blank = jnp.zeros((ref.shape[0], EDGE), ref.dtype)
        ref[:, :EDGE] = blank
        ref[:, EDGE + length:] = blank
    span = TILE + 2 * EDGE
    tapline[...] = jnp.zeros(tapline.shape, tapline.dtype)
    tapline[0:1, :n_taps] = taps_ref[...]
    line = jnp.broadcast_to(tapline[0:1, :], (TILE, span))
    band = pltpu.roll(line, EDGE - (n_taps - 1) // 2, 1, stride=1, stride_axis=0)
    band_high = band.astype(jnp.bfloat16)
    band_low = (band - band_high.astype(jnp.float32)).astype(jnp.bfloat16)
    ahead = lax.broadcasted_iota(jnp.int32, (TILE, span), 1) - lax.broadcasted_iota(jnp.int32, (TILE, span), 0) - EDGE
    box = jnp.where((ahead >= -AVG_HALF) & (ahead <= AVG_HALF), 1.0, 0.0).astype(jnp.bfloat16)

    for copy in copies:
        copy.wait()
    for t in range(0, length, TILE):
        window = raw[:, t:t + span]
        value = times_rows(window, band_high) + times_rows(window, band_low)
        filt[:, t:t + TILE] = value
        size = jnp.abs(value)
        top = size.astype(jnp.bfloat16)
        high[:, EDGE + t:EDGE + t + TILE] = top
        low[:, EDGE + t:EDGE + t + TILE] = (size - top.astype(jnp.float32)).astype(jnp.bfloat16)
    for t in range(0, length, TILE):
        total = times_rows(high[:, t:t + span], box) + times_rows(low[:, t:t + span], box)
        magnitude = total * (1.0 / (2 * AVG_HALF + 1)) + 1e-5
        normal = (filt[:, t:t + TILE] / magnitude).astype(jnp.bfloat16)
        raw[:, EDGE + t:EDGE + t + TILE] = normal

    factor = float(length) ** -0.5
    half_lags = (LAGS - 1) // 2
    own_wide = raw[paired:, :]

    def shifted(place, shift):
        partners[place * paired:(place + 1) * paired, :] = raw[:paired, EDGE + shift:EDGE + shift + length]

    shifted(0, -1)
    shifted(1, 0)
    results = []
    for g, bases in enumerate(base_groups()):
        before = bases[0] <= half_lags
        if bases[0] == half_lags + 1:
            shifted(2, 1)
        start = 0 if before else paired
        lags = (-1, 0) if before else (0, 1)
        top = sum(len(group) for group in base_groups()[:g]) * own_rows
        for i, l in enumerate(bases):
            begin = EDGE + half_lags - l
            toep[top + i * own_rows:top + (i + 1) * own_rows, :] = own_wide[:, begin:begin + length]
        rows = toep[top:top + len(bases) * own_rows, :]
        sums = (times_rows(rows, partners[start:start + 2 * paired, :]) * factor).astype(jnp.bfloat16)
        held_lags = []
        for i, l in enumerate(bases):
            for side, extra in enumerate(lags):
                if not 0 <= l + extra < LAGS:
                    continue
                held_lags.append(l + extra)
                for r in range(ROUNDS):
                    column = side * paired + r * block_rows
                    stage[r, l + extra] = sums[i * own_rows:(i + 1) * own_rows, column:column + block_rows]
        part = pl.ds(min(held_lags), len(held_lags))
        result = pltpu.make_async_copy(stage.at[:, part], out_ref.at[:, part], out_sem.at[g])
        result.start()
        results.append(result)
    for result in results:
        result.wait()


def correlate(everything, plan, taps):
    n_sta, n_tm, block_rows, cols = everything.shape
    length = n_tm * cols
    own_rows = block_rows // n_tm
    rows = ROUNDS * block_rows + own_rows
    wide = length + 2 * EDGE
    groups = base_groups()
    bf16 = jnp.bfloat16
    return pl.pallas_call(
        functools.partial(correlate_kernel, n_tm),
        out_shape=jax.ShapeDtypeStruct((ROUNDS, LAGS, own_rows, block_rows), bf16),
        in_specs=[
            pl.BlockSpec(memory_space=pltpu.SMEM),
            pl.BlockSpec(memory_space=pltpu.VMEM),
            pl.BlockSpec(memory_space=pl.ANY),
        ],
        out_specs=pl.BlockSpec(memory_space=pl.ANY),
        scratch_shapes=[
            pltpu.VMEM((rows, wide), bf16),
            pltpu.VMEM((8, TILE + 2 * EDGE), jnp.float32),
            pltpu.VMEM((rows, length), jnp.float32),
            pltpu.VMEM((rows, wide), bf16),
            pltpu.VMEM((rows, wide), bf16),
            pltpu.VMEM((3 * ROUNDS * block_rows, length), bf16),
            pltpu.VMEM((sum(map(len, groups)) * own_rows, length), bf16),
            pltpu.VMEM((ROUNDS, LAGS, own_rows, block_rows), bf16),
            pltpu.SemaphoreType.DMA((ROUNDS + 1, n_tm)),
            pltpu.SemaphoreType.DMA((len(groups),)),
        ],
        compiler_params=pltpu.CompilerParams(vmem_limit_bytes=60 * 2**20),
        name="correlate_blocks",
    )(plan, taps, everything)


def local(records, filter_taps, plan, station_valid):
    n_sta, n_tm = lax.axis_size("sta"), lax.axis_size("tm")
    everything = gather(records, station_valid[None, :], n_sta, n_tm)
    lagged = correlate(everything, plan, filter_taps[None, :])
    return jnp.transpose(lagged, (0, 2, 1, 3))


def solution(mesh):
    return jax.shard_map(
        local,
        mesh=mesh,
        in_specs=(P("sta", "tm"), P(), P(), P("sta")),
        out_specs=P(None, ("sta", "tm"), None, None),
        check_vma=False,
    )
```

```python
import functools

import jax
import jax.numpy as jnp
from jax import lax
from jax.experimental import pallas as pl
from jax.experimental.pallas import tpu as pltpu
from jax.sharding import PartitionSpec as P

AVG_HALF = 64
LAGS = 101
ROUNDS = 3
TILE = 256
EDGE = 128
BASE_GROUP = 13
MESH = pl.DeviceIdType.MESH


def flipped(index, mask):
    bit = 1
    while bit <= mask:
        if mask & bit:
            index = index + bit - 2 * bit * (lax.div(index, bit) % 2)
        bit *= 2
    return index


def gather_kernel(n_sta, n_tm, valid_ref, rec_ref, all_ref, valid, rec, held, in_sem, keep, z_send, z_recv, send, recv):
    sta = lax.axis_index("sta")
    tm = lax.axis_index("tm")
    bits = n_sta.bit_length() - 1
    outer = list(range(1, bits))

    def chunk_at(position):
        chunk = tm
        for here in range(n_tm):
            near = sorted(range(n_tm), key=lambda there: (abs(there - here), there))
            chunk = jnp.where(tm == here, near[position], chunk)
        return chunk

    chunks = [tm] + [chunk_at(position) for position in range(1, n_tm)]
    inputs = [
        pltpu.make_async_copy(valid_ref, valid, in_sem.at[0]),
        pltpu.make_async_copy(rec_ref, rec, in_sem.at[1]),
    ]
    for copy in inputs:
        copy.start()

    barrier = pltpu.get_barrier_semaphore()
    masks = [1] + list(range(2, n_sta, 2))
    for chunk in chunks[1:]:
        pl.semaphore_signal(barrier, inc=1, device_id=(sta, chunk), device_id_type=MESH)
    for mask in masks:
        pl.semaphore_signal(barrier, inc=1, device_id=(flipped(sta, mask), tm), device_id_type=MESH)

    for copy in inputs:
        copy.wait()
    rows = rec.shape[0]
    row = lax.broadcasted_iota(jnp.int32, (rows, rows), 0)
    col = lax.broadcasted_iota(jnp.int32, (rows, rows), 1)
    alive = jnp.where(row == col, valid[...], 0).astype(jnp.float32).astype(jnp.bfloat16)
    held[0, tm] = jnp.dot(alive, rec[...], preferred_element_type=jnp.float32).astype(jnp.bfloat16)

    pl.semaphore_wait(barrier, len(masks) + n_tm - 1)
    started = []
    kept = []

    def slot(mask, position):
        if mask & 1:
            return all_ref.at[flipped(sta, mask), chunks[position]]
        return held.at[mask // 2, chunks[position]]

    def pass_on(mask, position, jump):
        if jump & 1:
            target = all_ref.at[flipped(sta, mask), chunks[position]]
        else:
            target = held.at[(mask ^ jump) // 2, chunks[position]]
        copy = pltpu.make_async_remote_copy(
            src_ref=slot(mask, position),
            dst_ref=target,
            send_sem=send.at[mask ^ jump, position],
            recv_sem=recv.at[mask ^ jump, position],
            device_id=(flipped(sta, jump), tm),
            device_id_type=MESH,
        )
        copy.start()
        started.append(copy)

    def arrival(sem, mask, position):
        there = slot(mask, position)
        pltpu.make_async_copy(there, there, sem).wait()

    def to_core(mask, position):
        pass_on(mask, position, 1)
        copy = pltpu.make_async_copy(
            held.at[mask // 2, chunks[position]],
            all_ref.at[flipped(sta, mask), chunks[position]],
            keep.at[mask // 2, position],
        )
        copy.start()
        kept.append(copy)

    for position in range(1, n_tm):
        copy = pltpu.make_async_remote_copy(
            src_ref=held.at[0, tm],
            dst_ref=held.at[0, tm],
            send_sem=z_send.at[position],
            recv_sem=z_recv.at[tm],
            device_id=(sta, chunks[position]),
            device_id_type=MESH,
        )
        copy.start()
        started.append(copy)

    def direct(position):
        return position == n_tm - 1 or len(outer) != 2

    def first_bits(position):
        turn = position % 2
        return outer[turn:] + outer[:turn]

    def own_ready(position):
        if position:
            arrival(z_recv.at[chunks[position]], 0, position)
        if direct(position):
            for mask in range(2, n_sta, 2):
                pass_on(0, position, mask)
        else:
            for b in first_bits(position):
                pass_on(0, position, 1 << b)
        to_core(0, position)

    def neighbours(position):
        if not direct(position):
            first, second = first_bits(position)
            arrival(recv.at[1 << first, position], 1 << first, position)
            pass_on(1 << first, position, 1 << second)
            to_core(1 << first, position)
            arrival(recv.at[1 << second, position], 1 << second, position)
            to_core(1 << second, position)

    def far(position):
        for mask in range(2, n_sta, 2):
            if direct(position) or mask == sum(1 << b for b in outer):
                arrival(recv.at[mask, position], mask, position)
                to_core(mask, position)

    for turn in range(n_tm + 2):
        if turn < n_tm:
            own_ready(turn)
        if 1 <= turn <= n_tm:
            neighbours(turn - 1)
        if turn >= 2:
            far(turn - 2)
    for position in range(n_tm):
        for mask in range(1, n_sta, 2):
            arrival(recv.at[mask, position], mask, position)
    for copy in started:
        copy.wait_send()
    for copy in kept:
        copy.wait()


def gather(records, valid, n_sta, n_tm):
    rows, cols = records.shape
    half = max(n_sta // 2, 1)
    return pl.pallas_call(
        functools.partial(gather_kernel, n_sta, n_tm),
        out_shape=jax.ShapeDtypeStruct((n_sta, n_tm, rows, cols), records.dtype),
        in_specs=[pl.BlockSpec(memory_space=pl.ANY)] * 2,
        out_specs=pl.BlockSpec(memory_space=pl.ANY),
        scratch_shapes=[
            pltpu.VMEM(valid.shape, valid.dtype),
            pltpu.VMEM((rows, cols), records.dtype),
            pltpu.VMEM((half, n_tm, rows, cols), records.dtype),
            pltpu.SemaphoreType.DMA((2,)),
            pltpu.SemaphoreType.DMA((half, n_tm)),
            pltpu.SemaphoreType.DMA((n_tm,)),
            pltpu.SemaphoreType.DMA((n_tm,)),
            pltpu.SemaphoreType.DMA((n_sta, n_tm)),
            pltpu.SemaphoreType.DMA((n_sta, n_tm)),
        ],
        compiler_params=pltpu.CompilerParams(
            collective_id=0, has_side_effects=True, vmem_limit_bytes=60 * 2**20
        ),
        name="gather_records",
    )(valid, records)


def times_rows(left, right):
    return lax.dot_general(left, right, (((1,), (1,)), ((), ())), preferred_element_type=jnp.float32)


def base_groups():
    half = (LAGS - 1) // 2
    groups = []
    for bases in (list(range(half % 2, half + 1, 2)), list(range(half + 1, LAGS, 2))):
        groups += [bases[i:i + BASE_GROUP] for i in range(0, len(bases), BASE_GROUP)]
    return groups


def correlate_kernel(n_tm, plan_ref, taps_ref, all_ref, out_ref, raw, tapline, filt, high, low, partners, toep, stage, in_sem, out_sem):
    block_rows, cols = all_ref.shape[2], all_ref.shape[3]
    length = n_tm * cols
    own_rows = block_rows // n_tm
    n_taps = taps_ref.shape[1]
    paired = ROUNDS * block_rows
    sta = lax.axis_index("sta")
    first = pl.multiple_of(lax.axis_index("tm") * own_rows, own_rows)
    chunks = []
    for c in range(n_tm):
        lanes = pl.ds(EDGE + c * cols, cols)
        chunks.append([
            pltpu.make_async_copy(
                all_ref.at[jnp.bitwise_xor(plan_ref[r], sta), c],
                raw.at[pl.ds(r * block_rows, block_rows), lanes],
                in_sem.at[r, c],
            )
            for r in range(ROUNDS)
        ] + [
            pltpu.make_async_copy(
                all_ref.at[sta, c, pl.ds(first, own_rows), :],
                raw.at[pl.ds(paired, own_rows), lanes],
                in_sem.at[ROUNDS, c],
            )
        ])
        for copy in chunks[c]:
            copy.start()

    for ref in (raw, high, low):
        blank = jnp.zeros((ref.shape[0], EDGE), ref.dtype)
        ref[:, :EDGE] = blank
        ref[:, EDGE + length:] = blank
    span = TILE + 2 * EDGE
    tapline[...] = jnp.zeros(tapline.shape, tapline.dtype)
    tapline[0:1, :n_taps] = taps_ref[...]
    line = jnp.broadcast_to(tapline[0:1, :], (TILE, span))
    band = pltpu.roll(line, EDGE - (n_taps - 1) // 2, 1, stride=1, stride_axis=0)
    band_high = band.astype(jnp.bfloat16)
    band_low = (band - band_high.astype(jnp.float32)).astype(jnp.bfloat16)
    ahead = lax.broadcasted_iota(jnp.int32, (TILE, span), 1) - lax.broadcasted_iota(jnp.int32, (TILE, span), 0) - EDGE
    box = jnp.where((ahead >= -AVG_HALF) & (ahead <= AVG_HALF), 1.0, 0.0).astype(jnp.bfloat16)

    there = 0
    for t in range(0, length, TILE):
        while there < n_tm and there * cols < t + TILE + EDGE:
            for copy in chunks[there]:
                copy.wait()
            there += 1
        window = raw[:, t:t + span]
        value = times_rows(window, band_high) + times_rows(window, band_low)
        filt[:, t:t + TILE] = value
        size = jnp.abs(value)
        top = size.astype(jnp.bfloat16)
        high[:, EDGE + t:EDGE + t + TILE] = top
        low[:, EDGE + t:EDGE + t + TILE] = (size - top.astype(jnp.float32)).astype(jnp.bfloat16)
    for t in range(0, length, TILE):
        total = times_rows(high[:, t:t + span], box) + times_rows(low[:, t:t + span], box)
        magnitude = total * (1.0 / (2 * AVG_HALF + 1)) + 1e-5
        normal = (filt[:, t:t + TILE] / magnitude).astype(jnp.bfloat16)
        raw[:, EDGE + t:EDGE + t + TILE] = normal

    factor = float(length) ** -0.5
    half_lags = (LAGS - 1) // 2
    own_wide = raw[paired:, :]

    def shifted(place, shift):
        partners[place * paired:(place + 1) * paired, :] = raw[:paired, EDGE + shift:EDGE + shift + length]

    shifted(0, -1)
    shifted(1, 0)
    results = []
    for g, bases in enumerate(base_groups()):
        before = bases[0] <= half_lags
        if bases[0] == half_lags + 1:
            shifted(2, 1)
        start = 0 if before else paired
        lags = (-1, 0) if before else (0, 1)
        top = sum(len(group) for group in base_groups()[:g]) * own_rows
        for i, l in enumerate(bases):
            begin = EDGE + half_lags - l
            toep[top + i * own_rows:top + (i + 1) * own_rows, :] = own_wide[:, begin:begin + length]
        rows = toep[top:top + len(bases) * own_rows, :]
        sums = (times_rows(rows, partners[start:start + 2 * paired, :]) * factor).astype(jnp.bfloat16)
        held_lags = []
        for i, l in enumerate(bases):
            for side, extra in enumerate(lags):
                if not 0 <= l + extra < LAGS:
                    continue
                held_lags.append(l + extra)
                for r in range(ROUNDS):
                    column = side * paired + r * block_rows
                    stage[r, l + extra] = sums[i * own_rows:(i + 1) * own_rows, column:column + block_rows]
        part = pl.ds(min(held_lags), len(held_lags))
        result = pltpu.make_async_copy(stage.at[:, part], out_ref.at[:, part], out_sem.at[g])
        result.start()
        results.append(result)
    for result in results:
        result.wait()


def correlate(everything, plan, taps):
    n_sta, n_tm, block_rows, cols = everything.shape
    length = n_tm * cols
    own_rows = block_rows // n_tm
    rows = ROUNDS * block_rows + own_rows
    wide = length + 2 * EDGE
    groups = base_groups()
    bf16 = jnp.bfloat16
    return pl.pallas_call(
        functools.partial(correlate_kernel, n_tm),
        out_shape=jax.ShapeDtypeStruct((ROUNDS, LAGS, own_rows, block_rows), bf16),
        in_specs=[
            pl.BlockSpec(memory_space=pltpu.SMEM),
            pl.BlockSpec(memory_space=pltpu.VMEM),
            pl.BlockSpec(memory_space=pl.ANY),
        ],
        out_specs=pl.BlockSpec(memory_space=pl.ANY),
        scratch_shapes=[
            pltpu.VMEM((rows, wide), bf16),
            pltpu.VMEM((8, TILE + 2 * EDGE), jnp.float32),
            pltpu.VMEM((rows, length), jnp.float32),
            pltpu.VMEM((rows, wide), bf16),
            pltpu.VMEM((rows, wide), bf16),
            pltpu.VMEM((3 * ROUNDS * block_rows, length), bf16),
            pltpu.VMEM((sum(map(len, groups)) * own_rows, length), bf16),
            pltpu.VMEM((ROUNDS, LAGS, own_rows, block_rows), bf16),
            pltpu.SemaphoreType.DMA((ROUNDS + 1, n_tm)),
            pltpu.SemaphoreType.DMA((len(groups),)),
        ],
        compiler_params=pltpu.CompilerParams(vmem_limit_bytes=60 * 2**20),
        name="correlate_blocks",
    )(plan, taps, everything)


def local(records, filter_taps, plan, station_valid):
    n_sta, n_tm = lax.axis_size("sta"), lax.axis_size("tm")
    everything = gather(records, station_valid[None, :], n_sta, n_tm)
    lagged = correlate(everything, plan, filter_taps[None, :])
    return jnp.transpose(lagged, (0, 2, 1, 3))


def solution(mesh):
    return jax.shard_map(
        local,
        mesh=mesh,
        in_specs=(P("sta", "tm"), P(), P(), P("sta")),
        out_specs=P(None, ("sta", "tm"), None, None),
        check_vma=False,
    )
```

```python
import functools

import jax
import jax.numpy as jnp
from jax import lax
from jax.experimental import pallas as pl
from jax.experimental.pallas import tpu as pltpu
from jax.sharding import PartitionSpec as P

AVG_HALF = 64
LAGS = 101
ROUNDS = 3
TILE = 256
EDGE = 128
BASE_GROUP = 13
MESH = pl.DeviceIdType.MESH


def flipped(index, mask):
    bit = 1
    while bit <= mask:
        if mask & bit:
            index = index + bit - 2 * bit * (lax.div(index, bit) % 2)
        bit *= 2
    return index


def gather_kernel(n_sta, n_tm, valid_ref, rec_ref, all_ref, valid, rec, held, in_sem, keep, z_send, z_recv, send, recv):
    sta = lax.axis_index("sta")
    tm = lax.axis_index("tm")
    bits = n_sta.bit_length() - 1
    outer = list(range(1, bits))

    def chunk_at(position):
        chunk = tm
        for here in range(n_tm):
            near = sorted(range(n_tm), key=lambda there: (abs(there - here), there))
            chunk = jnp.where(tm == here, near[position], chunk)
        return chunk

    chunks = [tm] + [chunk_at(position) for position in range(1, n_tm)]
    inputs = [
        pltpu.make_async_copy(valid_ref, valid, in_sem.at[0]),
        pltpu.make_async_copy(rec_ref, rec, in_sem.at[1]),
    ]
    for copy in inputs:
        copy.start()

    barrier = pltpu.get_barrier_semaphore()
    masks = [1] + list(range(2, n_sta, 2))
    for chunk in chunks[1:]:
        pl.semaphore_signal(barrier, inc=1, device_id=(sta, chunk), device_id_type=MESH)
    for mask in masks:
        pl.semaphore_signal(barrier, inc=1, device_id=(flipped(sta, mask), tm), device_id_type=MESH)

    for copy in inputs:
        copy.wait()
    rows = rec.shape[0]
    row = lax.broadcasted_iota(jnp.int32, (rows, rows), 0)
    col = lax.broadcasted_iota(jnp.int32, (rows, rows), 1)
    alive = jnp.where(row == col, valid[...], 0).astype(jnp.float32).astype(jnp.bfloat16)
    held[0, tm] = jnp.dot(alive, rec[...], preferred_element_type=jnp.float32).astype(jnp.bfloat16)

    pl.semaphore_wait(barrier, len(masks) + n_tm - 1)
    started = []
    kept = []

    def slot(mask, position):
        if mask & 1:
            return all_ref.at[flipped(sta, mask), chunks[position]]
        return held.at[mask // 2, chunks[position]]

    def pass_on(mask, position, jump):
        if jump & 1:
            target = all_ref.at[flipped(sta, mask), chunks[position]]
        else:
            target = held.at[(mask ^ jump) // 2, chunks[position]]
        copy = pltpu.make_async_remote_copy(
            src_ref=slot(mask, position),
            dst_ref=target,
            send_sem=send.at[mask ^ jump, position],
            recv_sem=recv.at[mask ^ jump, position],
            device_id=(flipped(sta, jump), tm),
            device_id_type=MESH,
        )
        copy.start()
        started.append(copy)

    def arrival(sem, mask, position):
        there = slot(mask, position)
        pltpu.make_async_copy(there, there, sem).wait()

    def to_core(mask, position):
        pass_on(mask, position, 1)
        copy = pltpu.make_async_copy(
            held.at[mask // 2, chunks[position]],
            all_ref.at[flipped(sta, mask), chunks[position]],
            keep.at[mask // 2, position],
        )
        copy.start()
        kept.append(copy)

    for position in range(1, n_tm):
        copy = pltpu.make_async_remote_copy(
            src_ref=held.at[0, tm],
            dst_ref=held.at[0, tm],
            send_sem=z_send.at[position],
            recv_sem=z_recv.at[tm],
            device_id=(sta, chunks[position]),
            device_id_type=MESH,
        )
        copy.start()
        started.append(copy)

    def direct(position):
        return position == n_tm - 1 or len(outer) != 2

    def first_bits(position):
        turn = position % 2
        return outer[turn:] + outer[:turn]

    def own_ready(position):
        if position:
            arrival(z_recv.at[chunks[position]], 0, position)
        if direct(position):
            for mask in range(2, n_sta, 2):
                pass_on(0, position, mask)
        else:
            for b in first_bits(position):
                pass_on(0, position, 1 << b)
        to_core(0, position)

    def neighbours(position):
        if not direct(position):
            first, second = first_bits(position)
            arrival(recv.at[1 << first, position], 1 << first, position)
            pass_on(1 << first, position, 1 << second)
            to_core(1 << first, position)
            arrival(recv.at[1 << second, position], 1 << second, position)
            to_core(1 << second, position)

    def far(position):
        for mask in range(2, n_sta, 2):
            if direct(position) or mask == sum(1 << b for b in outer):
                arrival(recv.at[mask, position], mask, position)
                to_core(mask, position)

    for turn in range(n_tm + 2):
        if turn < n_tm:
            own_ready(turn)
        if 1 <= turn <= n_tm:
            neighbours(turn - 1)
        if turn >= 2:
            far(turn - 2)
    for position in range(n_tm):
        for mask in range(1, n_sta, 2):
            arrival(recv.at[mask, position], mask, position)
    for copy in started:
        copy.wait_send()
    for copy in kept:
        copy.wait()


def gather(records, valid, n_sta, n_tm):
    rows, cols = records.shape
    half = max(n_sta // 2, 1)
    return pl.pallas_call(
        functools.partial(gather_kernel, n_sta, n_tm),
        out_shape=jax.ShapeDtypeStruct((n_sta, n_tm, rows, cols), records.dtype),
        in_specs=[pl.BlockSpec(memory_space=pl.ANY)] * 2,
        out_specs=pl.BlockSpec(memory_space=pl.ANY),
        scratch_shapes=[
            pltpu.VMEM(valid.shape, valid.dtype),
            pltpu.VMEM((rows, cols), records.dtype),
            pltpu.VMEM((half, n_tm, rows, cols), records.dtype),
            pltpu.SemaphoreType.DMA((2,)),
            pltpu.SemaphoreType.DMA((half, n_tm)),
            pltpu.SemaphoreType.DMA((n_tm,)),
            pltpu.SemaphoreType.DMA((n_tm,)),
            pltpu.SemaphoreType.DMA((n_sta, n_tm)),
            pltpu.SemaphoreType.DMA((n_sta, n_tm)),
        ],
        compiler_params=pltpu.CompilerParams(
            collective_id=0, has_side_effects=True, vmem_limit_bytes=60 * 2**20
        ),
        name="gather_records",
    )(valid, records)


def times_rows(left, right):
    return lax.dot_general(left, right, (((1,), (1,)), ((), ())), preferred_element_type=jnp.float32)


def base_groups():
    half = (LAGS - 1) // 2
    groups = []
    for bases in (list(range(half % 2, half + 1, 2)), list(range(half + 1, LAGS, 2))):
        groups += [bases[i:i + BASE_GROUP] for i in range(0, len(bases), BASE_GROUP)]
    return groups


def correlate_kernel(n_tm, plan_ref, taps_ref, all_ref, out_ref, raw, tapline, filt, high, low, partners, toep, stage, in_sem, out_sem):
    block_rows, cols = all_ref.shape[2], all_ref.shape[3]
    length = n_tm * cols
    own_rows = block_rows // n_tm
    n_taps = taps_ref.shape[1]
    paired = ROUNDS * block_rows
    sta = lax.axis_index("sta")
    copies = []
    for r in range(ROUNDS):
        for c in range(n_tm):
            copies.append(pltpu.make_async_copy(
                all_ref.at[jnp.bitwise_xor(plan_ref[r], sta), c],
                raw.at[pl.ds(r * block_rows, block_rows), pl.ds(EDGE + c * cols, cols)],
                in_sem.at[r, c],
            ))
    first = pl.multiple_of(lax.axis_index("tm") * own_rows, own_rows)
    for c in range(n_tm):
        copies.append(pltpu.make_async_copy(
            all_ref.at[sta, c, pl.ds(first, own_rows), :],
            raw.at[pl.ds(paired, own_rows), pl.ds(EDGE + c * cols, cols)],
            in_sem.at[ROUNDS, c],
        ))
    for copy in copies:
        copy.start()

    for ref in (raw, high, low):
        blank = jnp.zeros((ref.shape[0], EDGE), ref.dtype)
        ref[:, :EDGE] = blank
        ref[:, EDGE + length:] = blank
    span = TILE + 2 * EDGE
    tapline[...] = jnp.zeros(tapline.shape, tapline.dtype)
    tapline[0:1, :n_taps] = taps_ref[...]
    line = jnp.broadcast_to(tapline[0:1, :], (TILE, span))
    band = pltpu.roll(line, EDGE - (n_taps - 1) // 2, 1, stride=1, stride_axis=0)
    band_high = band.astype(jnp.bfloat16)
    band_low = (band - band_high.astype(jnp.float32)).astype(jnp.bfloat16)
    ahead = lax.broadcasted_iota(jnp.int32, (TILE, span), 1) - lax.broadcasted_iota(jnp.int32, (TILE, span), 0) - EDGE
    box = jnp.where((ahead >= -AVG_HALF) & (ahead <= AVG_HALF), 1.0, 0.0).astype(jnp.bfloat16)

    for copy in copies:
        copy.wait()
    for t in range(0, length, TILE):
        window = raw[:, t:t + span]
        value = times_rows(window, band_high) + times_rows(window, band_low)
        filt[:, t:t + TILE] = value
        size = jnp.abs(value)
        top = size.astype(jnp.bfloat16)
        high[:, EDGE + t:EDGE + t + TILE] = top
        low[:, EDGE + t:EDGE + t + TILE] = (size - top.astype(jnp.float32)).astype(jnp.bfloat16)
    for t in range(0, length, TILE):
        total = times_rows(high[:, t:t + span], box) + times_rows(low[:, t:t + span], box)
        magnitude = total * (1.0 / (2 * AVG_HALF + 1)) + 1e-5
        normal = (filt[:, t:t + TILE] / magnitude).astype(jnp.bfloat16)
        raw[:, EDGE + t:EDGE + t + TILE] = normal

    factor = float(length) ** -0.5
    half_lags = (LAGS - 1) // 2
    own_wide = raw[paired:, :]

    def shifted(place, shift):
        partners[place * paired:(place + 1) * paired, :] = raw[:paired, EDGE + shift:EDGE + shift + length]

    shifted(0, -1)
    shifted(1, 0)
    groups = base_groups()

    def top_of(g):
        return sum(len(group) for group in groups[:g]) * own_rows

    def build(g):
        if groups[g][0] == half_lags + 1:
            shifted(2, 1)
        for i, l in enumerate(groups[g]):
            begin = EDGE + half_lags - l
            row = top_of(g) + i * own_rows
            toep[row:row + own_rows, :] = own_wide[:, begin:begin + length]

    results = []
    build(0)
    for g, bases in enumerate(groups):
        if g + 1 < len(groups):
            build(g + 1)
        before = bases[0] <= half_lags
        start = 0 if before else paired
        lags = (-1, 0) if before else (0, 1)
        top = top_of(g)
        rows = toep[top:top + len(bases) * own_rows, :]
        sums = (times_rows(rows, partners[start:start + 2 * paired, :]) * factor).astype(jnp.bfloat16)
        held_lags = []
        for i, l in enumerate(bases):
            for side, extra in enumerate(lags):
                if not 0 <= l + extra < LAGS:
                    continue
                held_lags.append(l + extra)
                for r in range(ROUNDS):
                    column = side * paired + r * block_rows
                    stage[r, l + extra] = sums[i * own_rows:(i + 1) * own_rows, column:column + block_rows]
        part = pl.ds(min(held_lags), len(held_lags))
        result = pltpu.make_async_copy(stage.at[:, part], out_ref.at[:, part], out_sem.at[g])
        result.start()
        results.append(result)
    for result in results:
        result.wait()


def correlate(everything, plan, taps):
    n_sta, n_tm, block_rows, cols = everything.shape
    length = n_tm * cols
    own_rows = block_rows // n_tm
    rows = ROUNDS * block_rows + own_rows
    wide = length + 2 * EDGE
    groups = base_groups()
    bf16 = jnp.bfloat16
    return pl.pallas_call(
        functools.partial(correlate_kernel, n_tm),
        out_shape=jax.ShapeDtypeStruct((ROUNDS, LAGS, own_rows, block_rows), bf16),
        in_specs=[
            pl.BlockSpec(memory_space=pltpu.SMEM),
            pl.BlockSpec(memory_space=pltpu.VMEM),
            pl.BlockSpec(memory_space=pl.ANY),
        ],
        out_specs=pl.BlockSpec(memory_space=pl.ANY),
        scratch_shapes=[
            pltpu.VMEM((rows, wide), bf16),
            pltpu.VMEM((8, TILE + 2 * EDGE), jnp.float32),
            pltpu.VMEM((rows, length), jnp.float32),
            pltpu.VMEM((rows, wide), bf16),
            pltpu.VMEM((rows, wide), bf16),
            pltpu.VMEM((3 * ROUNDS * block_rows, length), bf16),
            pltpu.VMEM((sum(map(len, groups)) * own_rows, length), bf16),
            pltpu.VMEM((ROUNDS, LAGS, own_rows, block_rows), bf16),
            pltpu.SemaphoreType.DMA((ROUNDS + 1, n_tm)),
            pltpu.SemaphoreType.DMA((len(groups),)),
        ],
        compiler_params=pltpu.CompilerParams(vmem_limit_bytes=60 * 2**20),
        name="correlate_blocks",
    )(plan, taps, everything)


def local(records, filter_taps, plan, station_valid):
    n_sta, n_tm = lax.axis_size("sta"), lax.axis_size("tm")
    everything = gather(records, station_valid[None, :], n_sta, n_tm)
    lagged = correlate(everything, plan, filter_taps[None, :])
    return jnp.transpose(lagged, (0, 2, 1, 3))


def solution(mesh):
    return jax.shard_map(
        local,
        mesh=mesh,
        in_specs=(P("sta", "tm"), P(), P(), P("sta")),
        out_specs=P(None, ("sta", "tm"), None, None),
        check_vma=False,
    )
```

```python
import functools

import jax
import jax.numpy as jnp
from jax import lax
from jax.experimental import pallas as pl
from jax.experimental.pallas import tpu as pltpu
from jax.sharding import PartitionSpec as P

AVG_HALF = 64
LAGS = 101
ROUNDS = 3
TILE = 256
EDGE = 128
BASE_GROUP = 13
MESH = pl.DeviceIdType.MESH


def flipped(index, mask):
    bit = 1
    while bit <= mask:
        if mask & bit:
            index = index + bit - 2 * bit * (lax.div(index, bit) % 2)
        bit *= 2
    return index


def gather_kernel(n_sta, n_tm, valid_ref, rec_ref, all_ref, valid, rec, held, in_sem, keep, z_send, z_recv, send, recv):
    sta = lax.axis_index("sta")
    tm = lax.axis_index("tm")
    bits = n_sta.bit_length() - 1
    outer = list(range(1, bits))

    def chunk_at(position):
        chunk = tm
        for here in range(n_tm):
            near = sorted(range(n_tm), key=lambda there: (abs(there - here), there))
            chunk = jnp.where(tm == here, near[position], chunk)
        return chunk

    chunks = [tm] + [chunk_at(position) for position in range(1, n_tm)]
    inputs = [
        pltpu.make_async_copy(valid_ref, valid, in_sem.at[0]),
        pltpu.make_async_copy(rec_ref, rec, in_sem.at[1]),
    ]
    for copy in inputs:
        copy.start()

    barrier = pltpu.get_barrier_semaphore()
    masks = [1] + list(range(2, n_sta, 2))
    for chunk in chunks[1:]:
        pl.semaphore_signal(barrier, inc=1, device_id=(sta, chunk), device_id_type=MESH)
    for mask in masks:
        pl.semaphore_signal(barrier, inc=1, device_id=(flipped(sta, mask), tm), device_id_type=MESH)

    for copy in inputs:
        copy.wait()
    rows = rec.shape[0]
    row = lax.broadcasted_iota(jnp.int32, (rows, rows), 0)
    col = lax.broadcasted_iota(jnp.int32, (rows, rows), 1)
    alive = jnp.where(row == col, valid[...], 0).astype(jnp.float32).astype(jnp.bfloat16)
    held[0, tm] = jnp.dot(alive, rec[...], preferred_element_type=jnp.float32).astype(jnp.bfloat16)

    pl.semaphore_wait(barrier, len(masks) + n_tm - 1)
    started = []
    kept = []

    def slot(mask, position):
        if mask & 1:
            return all_ref.at[flipped(sta, mask), chunks[position]]
        return held.at[mask // 2, chunks[position]]

    def pass_on(mask, position, jump):
        if jump & 1:
            target = all_ref.at[flipped(sta, mask), chunks[position]]
        else:
            target = held.at[(mask ^ jump) // 2, chunks[position]]
        copy = pltpu.make_async_remote_copy(
            src_ref=slot(mask, position),
            dst_ref=target,
            send_sem=send.at[mask ^ jump, position],
            recv_sem=recv.at[mask ^ jump, position],
            device_id=(flipped(sta, jump), tm),
            device_id_type=MESH,
        )
        copy.start()
        started.append(copy)

    def arrival(sem, mask, position):
        there = slot(mask, position)
        pltpu.make_async_copy(there, there, sem).wait()

    def to_core(mask, position):
        pass_on(mask, position, 1)
        copy = pltpu.make_async_copy(
            held.at[mask // 2, chunks[position]],
            all_ref.at[flipped(sta, mask), chunks[position]],
            keep.at[mask // 2, position],
        )
        copy.start()
        kept.append(copy)

    for position in range(1, n_tm):
        copy = pltpu.make_async_remote_copy(
            src_ref=held.at[0, tm],
            dst_ref=held.at[0, tm],
            send_sem=z_send.at[position],
            recv_sem=z_recv.at[tm],
            device_id=(sta, chunks[position]),
            device_id_type=MESH,
        )
        copy.start()
        started.append(copy)

    def direct(position):
        return len(outer) != 2

    def first_bits(position):
        turn = position % 2
        return outer[turn:] + outer[:turn]

    def own_ready(position):
        if position:
            arrival(z_recv.at[chunks[position]], 0, position)
        if direct(position):
            for mask in range(2, n_sta, 2):
                pass_on(0, position, mask)
        else:
            for b in first_bits(position):
                pass_on(0, position, 1 << b)
        to_core(0, position)

    def neighbours(position):
        if not direct(position):
            first, second = first_bits(position)
            arrival(recv.at[1 << first, position], 1 << first, position)
            pass_on(1 << first, position, 1 << second)
            to_core(1 << first, position)
            arrival(recv.at[1 << second, position], 1 << second, position)
            to_core(1 << second, position)

    def far(position):
        for mask in range(2, n_sta, 2):
            if direct(position) or mask == sum(1 << b for b in outer):
                arrival(recv.at[mask, position], mask, position)
                to_core(mask, position)

    for turn in range(n_tm + 2):
        if turn < n_tm:
            own_ready(turn)
        if 1 <= turn <= n_tm:
            neighbours(turn - 1)
        if turn >= 2:
            far(turn - 2)
    for position in range(n_tm):
        for mask in range(1, n_sta, 2):
            arrival(recv.at[mask, position], mask, position)
    for copy in started:
        copy.wait_send()
    for copy in kept:
        copy.wait()


def gather(records, valid, n_sta, n_tm):
    rows, cols = records.shape
    half = max(n_sta // 2, 1)
    return pl.pallas_call(
        functools.partial(gather_kernel, n_sta, n_tm),
        out_shape=jax.ShapeDtypeStruct((n_sta, n_tm, rows, cols), records.dtype),
        in_specs=[pl.BlockSpec(memory_space=pl.ANY)] * 2,
        out_specs=pl.BlockSpec(memory_space=pl.ANY),
        scratch_shapes=[
            pltpu.VMEM(valid.shape, valid.dtype),
            pltpu.VMEM((rows, cols), records.dtype),
            pltpu.VMEM((half, n_tm, rows, cols), records.dtype),
            pltpu.SemaphoreType.DMA((2,)),
            pltpu.SemaphoreType.DMA((half, n_tm)),
            pltpu.SemaphoreType.DMA((n_tm,)),
            pltpu.SemaphoreType.DMA((n_tm,)),
            pltpu.SemaphoreType.DMA((n_sta, n_tm)),
            pltpu.SemaphoreType.DMA((n_sta, n_tm)),
        ],
        compiler_params=pltpu.CompilerParams(
            collective_id=0, has_side_effects=True, vmem_limit_bytes=60 * 2**20
        ),
        name="gather_records",
    )(valid, records)


def times_rows(left, right):
    return lax.dot_general(left, right, (((1,), (1,)), ((), ())), preferred_element_type=jnp.float32)


def base_groups():
    half = (LAGS - 1) // 2
    groups = []
    for bases in (list(range(half % 2, half + 1, 2)), list(range(half + 1, LAGS, 2))):
        groups += [bases[i:i + BASE_GROUP] for i in range(0, len(bases), BASE_GROUP)]
    return groups


def correlate_kernel(n_tm, plan_ref, taps_ref, all_ref, out_ref, raw, tapline, filt, high, low, partners, toep, stage, in_sem, out_sem):
    block_rows, cols = all_ref.shape[2], all_ref.shape[3]
    length = n_tm * cols
    own_rows = block_rows // n_tm
    n_taps = taps_ref.shape[1]
    paired = ROUNDS * block_rows
    sta = lax.axis_index("sta")
    copies = []
    for r in range(ROUNDS):
        for c in range(n_tm):
            copies.append(pltpu.make_async_copy(
                all_ref.at[jnp.bitwise_xor(plan_ref[r], sta), c],
                raw.at[pl.ds(r * block_rows, block_rows), pl.ds(EDGE + c * cols, cols)],
                in_sem.at[r, c],
            ))
    first = pl.multiple_of(lax.axis_index("tm") * own_rows, own_rows)
    for c in range(n_tm):
        copies.append(pltpu.make_async_copy(
            all_ref.at[sta, c, pl.ds(first, own_rows), :],
            raw.at[pl.ds(paired, own_rows), pl.ds(EDGE + c * cols, cols)],
            in_sem.at[ROUNDS, c],
        ))
    for copy in copies:
        copy.start()

    for ref in (raw, high, low):
        blank = jnp.zeros((ref.shape[0], EDGE), ref.dtype)
        ref[:, :EDGE] = blank
        ref[:, EDGE + length:] = blank
    span = TILE + 2 * EDGE
    tapline[...] = jnp.zeros(tapline.shape, tapline.dtype)
    tapline[0:1, :n_taps] = taps_ref[...]
    line = jnp.broadcast_to(tapline[0:1, :], (TILE, span))
    band = pltpu.roll(line, EDGE - (n_taps - 1) // 2, 1, stride=1, stride_axis=0)
    band_high = band.astype(jnp.bfloat16)
    band_low = (band - band_high.astype(jnp.float32)).astype(jnp.bfloat16)
    ahead = lax.broadcasted_iota(jnp.int32, (TILE, span), 1) - lax.broadcasted_iota(jnp.int32, (TILE, span), 0) - EDGE
    box = jnp.where((ahead >= -AVG_HALF) & (ahead <= AVG_HALF), 1.0, 0.0).astype(jnp.bfloat16)

    for copy in copies:
        copy.wait()
    for t in range(0, length, TILE):
        window = raw[:, t:t + span]
        value = times_rows(window, band_high) + times_rows(window, band_low)
        filt[:, t:t + TILE] = value
        size = jnp.abs(value)
        top = size.astype(jnp.bfloat16)
        high[:, EDGE + t:EDGE + t + TILE] = top
        low[:, EDGE + t:EDGE + t + TILE] = (size - top.astype(jnp.float32)).astype(jnp.bfloat16)
    for t in range(0, length, TILE):
        total = times_rows(high[:, t:t + span], box) + times_rows(low[:, t:t + span], box)
        magnitude = total * (1.0 / (2 * AVG_HALF + 1)) + 1e-5
        normal = (filt[:, t:t + TILE] / magnitude).astype(jnp.bfloat16)
        raw[:, EDGE + t:EDGE + t + TILE] = normal

    factor = float(length) ** -0.5
    half_lags = (LAGS - 1) // 2
    own_wide = raw[paired:, :]

    def shifted(place, shift):
        partners[place * paired:(place + 1) * paired, :] = raw[:paired, EDGE + shift:EDGE + shift + length]

    shifted(0, -1)
    shifted(1, 0)
    results = []
    for g, bases in enumerate(base_groups()):
        before = bases[0] <= half_lags
        if bases[0] == half_lags + 1:
            shifted(2, 1)
        start = 0 if before else paired
        lags = (-1, 0) if before else (0, 1)
        top = sum(len(group) for group in base_groups()[:g]) * own_rows
        for i, l in enumerate(bases):
            begin = EDGE + half_lags - l
            toep[top + i * own_rows:top + (i + 1) * own_rows, :] = own_wide[:, begin:begin + length]
        rows = toep[top:top + len(bases) * own_rows, :]
        sums = (times_rows(rows, partners[start:start + 2 * paired, :]) * factor).astype(jnp.bfloat16)
        held_lags = []
        for i, l in enumerate(bases):
            for side, extra in enumerate(lags):
                if not 0 <= l + extra < LAGS:
                    continue
                held_lags.append(l + extra)
                for r in range(ROUNDS):
                    column = side * paired + r * block_rows
                    stage[r, l + extra] = sums[i * own_rows:(i + 1) * own_rows, column:column + block_rows]
        part = pl.ds(min(held_lags), len(held_lags))
        result = pltpu.make_async_copy(stage.at[:, part], out_ref.at[:, part], out_sem.at[g])
        result.start()
        results.append(result)
    for result in results:
        result.wait()


def correlate(everything, plan, taps):
    n_sta, n_tm, block_rows, cols = everything.shape
    length = n_tm * cols
    own_rows = block_rows // n_tm
    rows = ROUNDS * block_rows + own_rows
    wide = length + 2 * EDGE
    groups = base_groups()
    bf16 = jnp.bfloat16
    return pl.pallas_call(
        functools.partial(correlate_kernel, n_tm),
        out_shape=jax.ShapeDtypeStruct((ROUNDS, LAGS, own_rows, block_rows), bf16),
        in_specs=[
            pl.BlockSpec(memory_space=pltpu.SMEM),
            pl.BlockSpec(memory_space=pltpu.VMEM),
            pl.BlockSpec(memory_space=pl.ANY),
        ],
        out_specs=pl.BlockSpec(memory_space=pl.ANY),
        scratch_shapes=[
            pltpu.VMEM((rows, wide), bf16),
            pltpu.VMEM((8, TILE + 2 * EDGE), jnp.float32),
            pltpu.VMEM((rows, length), jnp.float32),
            pltpu.VMEM((rows, wide), bf16),
            pltpu.VMEM((rows, wide), bf16),
            pltpu.VMEM((3 * ROUNDS * block_rows, length), bf16),
            pltpu.VMEM((sum(map(len, groups)) * own_rows, length), bf16),
            pltpu.VMEM((ROUNDS, LAGS, own_rows, block_rows), bf16),
            pltpu.SemaphoreType.DMA((ROUNDS + 1, n_tm)),
            pltpu.SemaphoreType.DMA((len(groups),)),
        ],
        compiler_params=pltpu.CompilerParams(vmem_limit_bytes=60 * 2**20),
        name="correlate_blocks",
    )(plan, taps, everything)


def local(records, filter_taps, plan, station_valid):
    n_sta, n_tm = lax.axis_size("sta"), lax.axis_size("tm")
    everything = gather(records, station_valid[None, :], n_sta, n_tm)
    lagged = correlate(everything, plan, filter_taps[None, :])
    return jnp.transpose(lagged, (0, 2, 1, 3))


def solution(mesh):
    return jax.shard_map(
        local,
        mesh=mesh,
        in_specs=(P("sta", "tm"), P(), P(), P("sta")),
        out_specs=P(None, ("sta", "tm"), None, None),
        check_vma=False,
    )
```
